32 devices in a mesh: dp: 4 (over x, core), ctx: 8 (over z, y).
Axes of the slice: x: 2, y: 2, z: 4, core: 2. Of those that a mesh axis runs over, the one named last changes fastest.
Arguments:
- inputs: bfloat16 [8, 2048, 896], P('dp', 'ctx'), may hold values from -6 to 6
- cotangent: bfloat16 [8, 2048, 896], P('dp', 'ctx'), may hold values from -6 to 6
- lengths: int32 [8], P('dp'), may hold values from 256 to 2048, as said below
- qkv_weight: float32 [896, 1152], P(('dp', 'ctx')), may hold values from -0.1875 to 0.1875
- out_weight: float32 [896, 896], P(('dp', 'ctx')), may hold values from -2 to 2
- gate_up_weight: float32 [896, 9728], P(('dp', 'ctx')), may hold values from -0.1875 to 0.1875
- down_weight: float32 [4864, 896], P(('dp', 'ctx')), may hold values from -0.078125 to 0.078125
- gains_biases: float32 [2944], P(('dp', 'ctx')), may hold values from -2 to 2.5
- qkv_moment: float32 [896, 1152], P(('dp', 'ctx')), may hold values from -0.0004272461 to 0.0004272461
- qkv_square: float32 [896, 1152], P(('dp', 'ctx')), may hold values from 3.5272696e-09 to 1.4082255e-08
- out_moment: float32 [896, 896], P(('dp', 'ctx')), may hold values from -0.0004272461 to 0.0004272461
- out_square: float32 [896, 896], P(('dp', 'ctx')), may hold values from 3.5272696e-09 to 1.4082255e-08
- gate_up_moment: float32 [896, 9728], P(('dp', 'ctx')), may hold values from -0.0004272461 to 0.0004272461
- gate_up_square: float32 [896, 9728], P(('dp', 'ctx')), may hold values from 3.5272696e-09 to 1.4082255e-08
- down_moment: float32 [4864, 896], P(('dp', 'ctx')), may hold values from -0.0004272461 to 0.0004272461
- down_square: float32 [4864, 896], P(('dp', 'ctx')), may hold values from 3.5272696e-09 to 1.4082255e-08
- small_moment: float32 [2944], P(('dp', 'ctx')), may hold values from -0.0004272461 to 0.0004272461
- small_square: float32 [2944], P(('dp', 'ctx')), may hold values from 4.5130275e-07 to 1.8038698e-06
Outputs:
- output: bfloat16 [8, 2048, 896], P('dp', 'ctx')
- input_grad: bfloat16 [8, 2048, 896], P('dp', 'ctx')
- grad_norm: float32 [], replicated
- qkv_grad: float32 [896, 1152], P(('dp', 'ctx'))
- qkv_moment_new: float32 [896, 1152], P(('dp', 'ctx'))
- qkv_square_new: float32 [896, 1152], P(('dp', 'ctx'))
- qkv_weight_new: float32 [896, 1152], P(('dp', 'ctx'))
- out_grad: float32 [896, 896], P(('dp', 'ctx'))
- out_moment_new: float32 [896, 896], P(('dp', 'ctx'))
- out_square_new: float32 [896, 896], P(('dp', 'ctx'))
- out_weight_new: float32 [896, 896], P(('dp', 'ctx'))
- gate_up_grad: float32 [896, 9728], P(('dp', 'ctx'))
- gate_up_moment_new: float32 [896, 9728], P(('dp', 'ctx'))
- gate_up_square_new: float32 [896, 9728], P(('dp', 'ctx'))
- gate_up_weight_new: float32 [896, 9728], P(('dp', 'ctx'))
- down_grad: float32 [4864, 896], P(('dp', 'ctx'))
- down_moment_new: float32 [4864, 896], P(('dp', 'ctx'))
- down_square_new: float32 [4864, 896], P(('dp', 'ctx'))
- down_weight_new: float32 [4864, 896], P(('dp', 'ctx'))
- small_grad: float32 [2944], P(('dp', 'ctx'))
- small_moment_new: float32 [2944], P(('dp', 'ctx'))
- small_square_new: float32 [2944], P(('dp', 'ctx'))
- small_weight_new: float32 [2944], P(('dp', 'ctx'))
The draws below stay inside these ranges and needn't reach their ends.
Inputs may be any that keep to these rules, and one draw needn't show every extreme that they name: `lengths`: in each group of 2 sequences of one index of dp, one sequence has length exactly 2048.
All inputs are finite; a program needn't handle non-finite values.
Results may differ from the reference program's by a relative error of at most 0.018.
The reference program's roundings to bfloat16 on the way count: a program that leaves them out, or rounds other values in their place, can miss the bound.
Values may be sent and summed in bfloat16 or wider, within the bound.
No kernel may reach another device: no remote copies, remote signals or barrier semaphores. Data moves between devices by JAX's collectives and lax.ppermute only.
A program may use at most 256 MiB of HBM per device.

```python
import math
import jax
import jax.numpy as jnp
from jax import lax

D = 896
HEADS = 14
KVH = 2
HD = 64
FF = 4864
ROWS_DEV = 2
STEP = 5
QD = 896
KVD = 128
SMALL = 2944
PARAMS = 14912384
LEN = 2048
ROWS = 8


def draw_lengths(key, part):
    key = jax.random.fold_in(key, 11)
    first, second = jax.random.split(key)
    drawn = jax.random.randint(first, (ROWS,), LEN // 8, LEN + 1)
    chosen = jax.random.randint(second, (ROWS // ROWS_DEV,), 0, ROWS_DEV)
    slot = jnp.arange(ROWS) % ROWS_DEV
    owner = jnp.arange(ROWS) // ROWS_DEV
    return jnp.where(slot == chosen[owner], LEN, drawn).astype(jnp.int32)


def draw_gains_biases(key, part):
    key = jax.random.fold_in(key, 23)
    first, second = jax.random.split(key)
    ramp = jnp.arange(D, dtype=jnp.float32) / (D - 1)
    gains = (0.5 + ramp)[None, :] * jax.random.uniform(first, (2, D), jnp.float32, 0.8, 1.25)
    bias = 0.3 * jnp.clip(jax.random.normal(second, (QD + 2 * KVH * HD,), jnp.float32), -4.0, 4.0)
    return jnp.concatenate([gains.reshape(-1), bias]).astype(jnp.float32)


def block_levels(own_key, extent, pieces, low, high):
    gain, own = 1.0, jax.random.fold_in(own_key, 6)
    for position, shards_of in pieces:
        draws = jnp.exp(jax.random.uniform(jax.random.fold_in(own, position), (shards_of,), jnp.float32, low / len(pieces), high / len(pieces)))
        gain = gain * jnp.repeat(draws, extent[position] // shards_of).reshape([-1 if axis == position else 1 for axis in range(len(extent))])
    return gain


def bell_draw(stream_key, extent, spread, limit, cuts=(), held_as=jnp.bfloat16):
    gain = block_levels(stream_key, extent, cuts, -0.22, 0.18) if cuts else 1.0
    values = jax.random.normal(stream_key, extent, jnp.float32) * spread * gain
    return jnp.minimum(jnp.maximum(values, -limit), limit).astype(held_as)


def setup_inputs(seed: int = 0) -> dict:
    streams_of = jax.random.split(jax.random.key(seed), 19)
    return {
        "inputs": bell_draw(streams_of[0], (ROWS, LEN, D), 1.0, 6.0, ((0, 4), (1, 8))),
        "cotangent": bell_draw(streams_of[1], (ROWS, LEN, D), 1.0, 6.0, ((0, 4), (1, 8))),
        "lengths": draw_lengths(jax.random.fold_in(streams_of[18], 71), 0),
        "qkv_weight": bell_draw(streams_of[3], (D, QD + 2 * KVD), D ** -0.5, 0.1875, ((0, 32),), jnp.float32),
        "out_weight": bell_draw(streams_of[4], (QD, D), (max(QD * 16 // LEN, 1)) ** -0.5, 2.0, ((0, 32),), jnp.float32),
        "gate_up_weight": bell_draw(streams_of[5], (D, 2 * FF), D ** -0.5, 0.1875, ((0, 32),), jnp.float32),
        "down_weight": bell_draw(streams_of[6], (FF, D), FF ** -0.5, 0.078125, ((0, 32),), jnp.float32),
        "gains_biases": draw_gains_biases(jax.random.fold_in(streams_of[18], 71), 0),
        "qkv_moment": bell_draw(streams_of[8], (D, QD + 2 * KVD), (0.111 / PARAMS ** 0.5), 0.0004272461, ((0, 32),), jnp.float32),
        "qkv_square": jnp.clip(jnp.exp(math.log(1.4082255361813623e-08) - 1.3843914 * jax.random.uniform(streams_of[9], (D, QD + 2 * KVD), jnp.float32) ** block_levels(streams_of[9], (D, QD + 2 * KVD), ((0, 32),), -0.2, 0.2)), 3.5272695875221416e-09, 1.4082255361813623e-08),
        "out_moment": bell_draw(streams_of[10], (QD, D), (0.111 / PARAMS ** 0.5), 0.0004272461, ((0, 32),), jnp.float32),
        "out_square": jnp.clip(jnp.exp(math.log(1.4082255361813623e-08) - 1.3843914 * jax.random.uniform(streams_of[11], (QD, D), jnp.float32) ** block_levels(streams_of[11], (QD, D), ((0, 32),), -0.2, 0.2)), 3.5272695875221416e-09, 1.4082255361813623e-08),
        "gate_up_moment": bell_draw(streams_of[12], (D, 2 * FF), (0.111 / PARAMS ** 0.5), 0.0004272461, ((0, 32),), jnp.float32),
        "gate_up_square": jnp.clip(jnp.exp(math.log(1.4082255361813623e-08) - 1.3843914 * jax.random.uniform(streams_of[13], (D, 2 * FF), jnp.float32) ** block_levels(streams_of[13], (D, 2 * FF), ((0, 32),), -0.2, 0.2)), 3.5272695875221416e-09, 1.4082255361813623e-08),
        "down_moment": bell_draw(streams_of[14], (FF, D), (0.111 / PARAMS ** 0.5), 0.0004272461, ((0, 32),), jnp.float32),
        "down_square": jnp.clip(jnp.exp(math.log(1.4082255361813623e-08) - 1.3843914 * jax.random.uniform(streams_of[15], (FF, D), jnp.float32) ** block_levels(streams_of[15], (FF, D), ((0, 32),), -0.2, 0.2)), 3.5272695875221416e-09, 1.4082255361813623e-08),
        "small_moment": bell_draw(streams_of[16], (SMALL,), (0.111 / PARAMS ** 0.5), 0.0004272461, ((0, 32),), jnp.float32),
        "small_square": jnp.clip(jnp.exp(math.log(1.8038698499367456e-06) - 1.3855511 * jax.random.uniform(streams_of[17], (SMALL,), jnp.float32) ** block_levels(streams_of[17], (SMALL,), ((0, 32),), -0.2, 0.2)), 4.513027533903369e-07, 1.8038698499367456e-06),
    }


EPS = 1e-06
NEG = -1e+30
BASE = 1000000.0
CLIP = 1.0
BETA_ONE = 0.9
BETA_TWO = 0.95
ADAM_EPS = 1e-08
RATES = (0.06, 1.0, 0.06, 0.03, 3.0)
DECAYS = (0.1, 0.1, 0.1, 0.1, 0.0)
HIGH = lax.Precision.HIGHEST

@jax.custom_vjp
def low(v):
    return lax.optimization_barrier(v.astype(jnp.bfloat16)).astype(jnp.float32)

@jax.custom_vjp
def low_back(v):
    return v

def low_keep(v):
    return (low(v), None)

def low_pass(kept, grad):
    return (grad,)

def back_keep(v):
    return (v, None)

def back_low(kept, grad):
    return (low(grad),)
low.defvjp(low_keep, low_pass)
low_back.defvjp(back_keep, back_low)

def rotate(tensor, positions, sign):
    half = tensor.shape[-1] // 2
    freq = jnp.exp(jnp.arange(half, dtype=jnp.float32) * (-2.0 * math.log(BASE) / tensor.shape[-1]))
    angle = positions.astype(jnp.float32)[:, None] * freq[None, :]
    cosine = jnp.cos(angle)[:, None, :]
    sine = sign * jnp.sin(angle)[:, None, :]
    first = tensor[..., :half]
    second = tensor[..., half:]
    return jnp.concatenate([first * cosine - second * sine, second * cosine + first * sine], -1)

def attend(query, key_rows, value_rows, length):
    total = query.shape[0]
    block = math.gcd(total, 512)
    group = HEADS // KVH
    key_pos = jnp.arange(total, dtype=jnp.int32)
    scale = HD ** (-0.5)

    def one_block(inputs_pair):
        rows_part, start = inputs_pair
        grouped = rows_part.reshape(block, KVH, group, HD)
        scores = jnp.einsum('qhgd,khd->hgqk', grouped, key_rows, precision=HIGH) * scale
        scores = low_back(scores)
        query_pos = start + jnp.arange(block, dtype=jnp.int32)
        allowed = (key_pos[None, :] <= query_pos[:, None]) & (key_pos[None, :] < length)
        scores = jnp.where(allowed[None, None], scores, NEG)
        probs = jax.nn.softmax(scores, axis=-1)
        result = jnp.einsum('hgqk,khd->qhgd', low(probs), value_rows, precision=HIGH)
        return result.reshape(block, HEADS, HD)
    blocks = query.reshape(total // block, block, HEADS, HD)
    starts = jnp.arange(total // block, dtype=jnp.int32) * block
    result = lax.map(jax.checkpoint(one_block), (blocks, starts))
    return result.reshape(total, HEADS, HD)

def layer_row(x_row, qkv_weight, out_weight, gate_up_weight, down_weight, gains_biases, length):
    total = x_row.shape[0]
    positions = jnp.arange(total, dtype=jnp.int32)
    kv_width = KVH * HD
    small = low(gains_biases)
    gain_attn = small[:D]
    gain_mlp = small[D:2 * D]
    bias = small[2 * D:]
    inverse_attn = lax.rsqrt(lax.optimization_barrier(jnp.mean(x_row * x_row, -1, keepdims=True)) + EPS)
    normed = low(x_row * inverse_attn * gain_attn)
    qkv = low_back(jnp.dot(normed, low(qkv_weight), precision=HIGH) + bias)
    query = low(rotate(qkv[:, :QD].reshape(total, HEADS, HD), positions, 1.0))
    key_rows = low(rotate(qkv[:, QD:QD + kv_width].reshape(total, KVH, HD), positions, 1.0))
    value_rows = low(qkv[:, QD + kv_width:].reshape(total, KVH, HD))
    attended = attend(query, key_rows, value_rows, length).reshape(total, QD)
    mixed = low(low_back(attended))
    hidden_state = x_row + low_back(jnp.dot(mixed, low(out_weight), precision=HIGH))
    inverse_mlp = lax.rsqrt(lax.optimization_barrier(jnp.mean(hidden_state * hidden_state, -1, keepdims=True)) + EPS)
    normed2 = low(hidden_state * inverse_mlp * gain_mlp)
    gate_up = low_back(jnp.dot(normed2, low(gate_up_weight), precision=HIGH))
    gate = gate_up[:, :FF]
    up_part = gate_up[:, FF:]
    inner = low(jax.nn.silu(gate) * up_part)
    return hidden_state + low_back(jnp.dot(inner, low(down_weight), precision=HIGH))

def add_pair(first_term, second_term):
    return first_term + second_term

def adam_step(gradient, moment, square, weight, factor, rate, decay):
    gradient = gradient * factor
    moment = BETA_ONE * moment + (1.0 - BETA_ONE) * gradient
    square = BETA_TWO * square + (1.0 - BETA_TWO) * gradient * gradient
    corr_one = 1.0 - BETA_ONE ** STEP
    corr_two = 1.0 - BETA_TWO ** STEP
    update = moment / corr_one / (jnp.sqrt(square / corr_two) + ADAM_EPS)
    weight = weight * (1.0 - rate * decay) - rate * update
    return (gradient, moment, square, weight)

def reference(inputs, cotangent, lengths, qkv_weight, out_weight, gate_up_weight, down_weight, gains_biases, qkv_moment, qkv_square, out_moment, out_square, gate_up_moment, gate_up_square, down_moment, down_square, small_moment, small_square):
    masters = (qkv_weight, out_weight, gate_up_weight, down_weight, gains_biases)
    positions = jnp.arange(LEN, dtype=jnp.int32)

    def per_row(totals, row):
        x_row, dy_row, length = row
        valid = (positions < length).astype(jnp.float32)[:, None]

        def forward(x_value, params):
            return layer_row(x_value, params[0], params[1], params[2], params[3], params[4], length)
        result, pull = jax.vjp(forward, x_row.astype(jnp.float32), masters)
        dx_row, grads = pull(dy_row.astype(jnp.float32) * valid)
        totals = jax.tree.map(add_pair, totals, grads)
        return (totals, (result.astype(jnp.bfloat16), dx_row.astype(jnp.bfloat16)))
    zeros = jax.tree.map(jnp.zeros_like, masters)
    grads, (output, input_grad) = lax.scan(per_row, zeros, (inputs, cotangent, lengths))
    square_sum = jnp.float32(0.0)
    for item in grads:
        square_sum = square_sum + jnp.sum(item * item)
    grad_norm = jnp.sqrt(square_sum)
    factor = CLIP / jnp.maximum(grad_norm, CLIP)
    qkv_new = adam_step(grads[0], qkv_moment, qkv_square, qkv_weight, factor, RATES[0], DECAYS[0])
    out_new = adam_step(grads[1], out_moment, out_square, out_weight, factor, RATES[1], DECAYS[1])
    gu_new = adam_step(grads[2], gate_up_moment, gate_up_square, gate_up_weight, factor, RATES[2], DECAYS[2])
    down_new = adam_step(grads[3], down_moment, down_square, down_weight, factor, RATES[3], DECAYS[3])
    small_new = adam_step(grads[4], small_moment, small_square, gains_biases, factor, RATES[4], DECAYS[4])
    return (output, input_grad, grad_norm, qkv_new[0], qkv_new[1], qkv_new[2], qkv_new[3], out_new[0], out_new[1], out_new[2], out_new[3], gu_new[0], gu_new[1], gu_new[2], gu_new[3], down_new[0], down_new[1], down_new[2], down_new[3], small_new[0], small_new[1], small_new[2], small_new[3])
```

```python
import functools
import math

import jax
import jax.numpy as jnp
from jax import lax
from jax.experimental import pallas as pl
from jax.experimental.pallas import tpu as pltpu
from jax.sharding import Mesh
from jax.sharding import PartitionSpec as P

D = 896
HEADS = 14
KVH = 2
HD = 64
FF = 4864
STEP = 5
QD = 896


EPS = 1e-06
NEG = -1e30
BASE = 1000000.0
CLIP = 1.0
BETA_ONE = 0.9
BETA_TWO = 0.95
ADAM_EPS = 1e-08
RATES = (0.06, 1.0, 0.06, 0.03, 3.0)
DECAYS = (0.1, 0.1, 0.1, 0.1, 0.0)


def across_tokens(left, right):
    flat_left = left.reshape(-1, left.shape[-1])
    flat_right = right.reshape(-1, right.shape[-1])
    return lax.dot_general(
        flat_left, flat_right, (((0,), (0,)), ((), ())), preferred_element_type=jnp.float32
    )


def against_weight(values, weight):
    return lax.dot_general(
        values, weight, (((values.ndim - 1,), (1,)), ((), ())), preferred_element_type=jnp.float32
    )


def norm_back(state, inverse, gain, upstream):
    scaled = gain * upstream
    change = inverse * scaled - state * inverse**3 * jnp.mean(scaled * state, -1, keepdims=True)
    gain_grad = jnp.sum((upstream * state * inverse).reshape(-1, state.shape[-1]), 0)
    return (change, gain_grad)


def adam_step(gradient, moment, square, weight, factor, rate, decay):
    gradient = gradient * factor
    moment = BETA_ONE * moment + (1.0 - BETA_ONE) * gradient
    square = BETA_TWO * square + (1.0 - BETA_TWO) * gradient * gradient
    corr_one = 1.0 - BETA_ONE**STEP
    corr_two = 1.0 - BETA_TWO**STEP
    update = moment / corr_one / (jnp.sqrt(square / corr_two) + ADAM_EPS)
    weight = weight * (1.0 - rate * decay) - rate * update
    return (gradient, moment, square, weight)


def swap(axis, value, count, step):
    return lax.ppermute(value, axis, [(i, i ^ step) for i in range(count)])


def pick(array, index, dim=0):
    return lax.dynamic_index_in_dim(array, index, dim, keepdims=False)


def place(pieces, index):
    out = jnp.zeros((len(pieces),) + pieces[0].shape, pieces[0].dtype)
    for step, piece in enumerate(pieces):
        out = lax.dynamic_update_index_in_dim(out, piece, index ^ step, 0)
    return out


def gather_axis(value, axis, count, up_only=False):
    index = lax.axis_index(axis)
    pieces = [value]
    for step in range(1, count):
        routes = [(i, i ^ step) for i in range(count) if i < i ^ step or not up_only]
        pieces.append(lax.ppermute(value, axis, routes))
    return place(pieces, index)


def add_up(parts):
    total = parts[0].astype(jnp.float32)
    for part in parts[1:]:
        total = total + part.astype(jnp.float32)
    return total.astype(jnp.bfloat16)


def reduce_axis(array, axis, dim, count, down_only=False):
    index = lax.axis_index(axis)
    total = pick(array, index, dim).astype(jnp.float32)
    for step in range(1, count):
        routes = [(i, i ^ step) for i in range(count) if i ^ step < i or not down_only]
        part = lax.ppermute(pick(array, index ^ step, dim), axis, routes)
        total = total + part.astype(jnp.float32)
    return total


def hold(*values):
    return lax.optimization_barrier(values)


def to_owners(grad, sizes):
    xs, zs, ys = sizes
    grad = grad.reshape(xs, 2, zs, *grad.shape[1:])
    grad = reduce_axis(grad, "core", 1, 2).astype(jnp.bfloat16)
    grad = reduce_axis(grad, "x", 0, xs).astype(jnp.bfloat16)
    return reduce_axis(grad, "z", 0, zs).astype(jnp.bfloat16)


def tree_sum(value, axis, count):
    terms = [value] + [swap(axis, value, count, step) for step in range(1, count)]
    while len(terms) > 1:
        terms = [terms[i] + terms[i + 1] for i in range(0, len(terms), 2)]
    return terms[0]


def across(left, right, left_dim, right_dim):
    return lax.dot_general(
        left, right, (((left_dim,), (right_dim,)), ((), ())), preferred_element_type=jnp.float32
    )


def rotation(positions, rows):
    half = HD // 2
    freq = jnp.exp(jnp.arange(half, dtype=jnp.float32) * (-2.0 * math.log(BASE) / HD))
    angle = jnp.tile(freq[:, None] * positions.astype(jnp.float32)[None, :], (1, rows))
    return (jnp.cos(angle), jnp.sin(angle))


def turn(tensor, angles, sign):
    cosine, sine = angles[0], sign * angles[1]
    first, second = jnp.split(tensor.reshape(-1, 2, HD // 2, tensor.shape[-1]), 2, 1)
    return jnp.concatenate(
        [first * cosine - second * sine, second * cosine + first * sine], 1
    ).reshape(tensor.shape)


def attend_kernel(group, block, meta, q_ref, kv_ref, out_ref, log_ref, top, total, accum):
    ctx, length = meta[0], meta[1 + pl.program_id(1)]
    blocks_y = kv_ref.shape[0]
    top[...] = jnp.full(top.shape, NEG, jnp.float32)
    total[...] = jnp.zeros(total.shape, jnp.float32)
    accum[...] = jnp.zeros(accum.shape, jnp.float32)

    def step(index, masked):
        pair = kv_ref[index % blocks_y, index // blocks_y, 0, 0]
        keys = pair[:, :HD]
        values = pair.T[HD:]
        if masked:
            key_pos = index * block + lax.broadcasted_iota(jnp.int32, (block, block), 0)
            query_pos = ctx * block + lax.broadcasted_iota(jnp.int32, (block, block), 1)
            allowed = (key_pos <= query_pos) & (key_pos < length)
        heads = range(group)
        span = [slice(head * HD, (head + 1) * HD) for head in heads]
        scores = [
            jnp.dot(keys, q_ref[span[head]], preferred_element_type=jnp.float32) for head in heads
        ]
        if masked:
            scores = [jnp.where(allowed, part, NEG) for part in scores]
        old = top[...]
        new = jnp.maximum(
            old, jnp.concatenate([jnp.max(part, 0, keepdims=True) for part in scores], 0)
        )
        factor = jnp.exp(old - new)
        top[...] = new
        probs = [jnp.exp(scores[head] - new[head : head + 1]) for head in heads]
        total[...] = total[...] * factor + jnp.concatenate(
            [jnp.sum(part, 0, keepdims=True) for part in probs], 0
        )
        weighted = [
            jnp.dot(values, part.astype(jnp.bfloat16), preferred_element_type=jnp.float32)
            for part in probs
        ]
        for head in heads:
            accum[span[head]] = accum[span[head]] * factor[head : head + 1] + weighted[head]

    clear = jnp.minimum(ctx, length // block)
    last = jnp.minimum(ctx + 1, (length + block - 1) // block)
    pl.loop(0, clear)(lambda index: step(index, False))
    pl.loop(clear, last)(lambda index: step(index, True))
    for head in range(group):
        rows = slice(head * HD, (head + 1) * HD)
        out_ref[rows] = accum[rows] / total[head : head + 1]
    log_ref[0] = top[...] + jnp.log(total[...])


def attend_back_kernel(
    group, block, meta, q_ref, g_ref, out_ref, log_ref, kv_ref, dq_ref, dkv_ref, both, delta
):
    ctx, length = meta[0], meta[1 + pl.program_id(0)]
    blocks_y, blocks_z = kv_ref.shape[0], kv_ref.shape[1]
    dq_ref[...] = jnp.zeros(dq_ref.shape, jnp.float32)
    for head in range(group):
        rows = slice(head * HD, (head + 1) * HD)
        query, upper = q_ref[rows], g_ref[rows]
        both[head] = jnp.concatenate([query, upper], 0).T
        delta[head : head + 1] = jnp.sum(upper.astype(jnp.float32) * out_ref[rows], 0, keepdims=True)
    lane = lax.broadcasted_iota(jnp.int32, (block, 2 * HD), 1)

    def step(index, masked):
        pair = kv_ref[index % blocks_y, index // blocks_y, 0, 0]
        keys, values = pair[:, :HD], pair[:, HD:]
        keys_across = pair.T[:HD]
        if masked:
            key_pos = index * block + lax.broadcasted_iota(jnp.int32, (block, block), 0)
            query_pos = ctx * block + lax.broadcasted_iota(jnp.int32, (block, block), 1)
            allowed = (key_pos <= query_pos) & (key_pos < length)
        d_keys = jnp.zeros((block, 2 * HD), jnp.float32)
        d_values = jnp.zeros((block, 2 * HD), jnp.float32)
        heads = range(group)
        span = [slice(head * HD, (head + 1) * HD) for head in heads]
        scores = [
            jnp.dot(keys, q_ref[span[head]], preferred_element_type=jnp.float32) for head in heads
        ]
        d_probs = [
            jnp.dot(values, g_ref[span[head]], preferred_element_type=jnp.float32) for head in heads
        ]
        probs = [jnp.exp(scores[head] - log_ref[0, head : head + 1]) for head in heads]
        if masked:
            probs = [jnp.where(allowed, part, 0.0) for part in probs]
        d_scores = [
            (probs[head] * (d_probs[head] - delta[head : head + 1])).astype(jnp.bfloat16)
            for head in heads
        ]
        probs = [part.astype(jnp.bfloat16) for part in probs]
        d_query = [
            jnp.dot(keys_across, part, preferred_element_type=jnp.float32) for part in d_scores
        ]
        for head in heads:
            d_keys += jnp.dot(d_scores[head], both[head], preferred_element_type=jnp.float32)
        for head in heads:
            d_values += jnp.dot(probs[head], both[head], preferred_element_type=jnp.float32)
        for head in heads:
            dq_ref[span[head]] += d_query[head]
        merged = jnp.where(lane < HD, d_keys, d_values)
        dkv_ref[index % blocks_y, index // blocks_y, 0] = merged.astype(jnp.bfloat16)

    clear = jnp.minimum(ctx, length // block)
    last = jnp.minimum(ctx + 1, (length + block - 1) // block)
    pl.loop(0, clear)(lambda index: step(index, False))
    pl.loop(clear, last)(lambda index: step(index, True))

    @pl.loop(last, blocks_y * blocks_z)
    def _(index):
        dkv_ref[index % blocks_y, index // blocks_y, 0] = jnp.zeros(
            (block, 2 * HD), jnp.bfloat16
        )


def attention(meta, query, all_kv, block):
    ys, zs, _, rows, _, _ = all_kv.shape
    group = HEADS // KVH
    wide = pl.BlockSpec((group * HD, block), lambda h, r, meta: (h, r))
    pairs = pl.BlockSpec((ys, zs, 1, 1, block, 2 * HD), lambda h, r, meta: (0, 0, h, r, 0, 0))
    logs = pl.BlockSpec((1, group, block), lambda h, r, meta: (h, 0, r))
    work = rows * HEADS * block * ys * zs * block
    return pl.pallas_call(
        functools.partial(attend_kernel, group, block),
        grid_spec=pltpu.PrefetchScalarGridSpec(
            num_scalar_prefetch=1,
            grid=(KVH, rows),
            in_specs=[wide, pairs],
            out_specs=[wide, logs],
            scratch_shapes=[
                pltpu.VMEM((group, block), jnp.float32),
                pltpu.VMEM((group, block), jnp.float32),
                pltpu.VMEM((group * HD, block), jnp.float32),
            ],
        ),
        out_shape=[
            jax.ShapeDtypeStruct((QD, rows * block), jnp.float32),
            jax.ShapeDtypeStruct((KVH, group, rows * block), jnp.float32),
        ],
        compiler_params=pltpu.CompilerParams(vmem_limit_bytes=32 * 2**20),
        cost_estimate=pl.CostEstimate(
            flops=4 * work * HD, bytes_accessed=4 * all_kv.size, transcendentals=work
        ),
        name="attend",
    )(meta, query, all_kv)


def attention_back(h, meta, query, upper, attended, logs, all_kv, block):
    ys, zs, _, rows, _, _ = all_kv.shape
    group = HEADS // KVH
    wide = pl.BlockSpec((group * HD, block), lambda r, meta: (h, r))
    narrow = pl.BlockSpec((group * HD, block), lambda r, meta: (0, r))
    pairs = pl.BlockSpec((ys, zs, 1, 1, block, 2 * HD), lambda r, meta: (0, 0, h, r, 0, 0))
    terms = pl.BlockSpec((ys, zs, 1, block, 2 * HD), lambda r, meta: (0, 0, r, 0, 0))
    log_spec = pl.BlockSpec((1, group, block), lambda r, meta: (h, 0, r))
    work = rows * group * block * ys * zs * block
    return pl.pallas_call(
        functools.partial(attend_back_kernel, group, block),
        grid_spec=pltpu.PrefetchScalarGridSpec(
            num_scalar_prefetch=1,
            grid=(rows,),
            in_specs=[wide, wide, wide, log_spec, pairs],
            out_specs=[narrow, terms],
            scratch_shapes=[
                pltpu.VMEM((group, block, 2 * HD), jnp.bfloat16),
                pltpu.VMEM((group, block), jnp.float32),
            ],
        ),
        out_shape=[
            jax.ShapeDtypeStruct((group * HD, rows * block), jnp.float32),
            jax.ShapeDtypeStruct((ys, zs, rows, block, 2 * HD), jnp.bfloat16),
        ],
        compiler_params=pltpu.CompilerParams(vmem_limit_bytes=32 * 2**20),
        cost_estimate=pl.CostEstimate(
            flops=10 * work * HD, bytes_accessed=4 * all_kv.size, transcendentals=work
        ),
        name="attend_back",
    )(meta, query, upper, attended, logs, all_kv)


def layer(
    sizes,
    inputs,
    cotangent,
    lengths,
    qkv_weight,
    out_weight,
    gate_up_weight,
    down_weight,
    gains_biases,
    qkv_moment,
    qkv_square,
    out_moment,
    out_square,
    gate_up_moment,
    gate_up_square,
    down_moment,
    down_square,
    small_moment,
    small_square,
):
    xs, zs, ys = sizes
    everyone = ("x", "core", "z", "y")
    chips = ("x", "z", "y")
    low = jnp.bfloat16
    rows, block_len, width = inputs.shape
    tokens = rows * block_len
    core, y_index = lax.axis_index("core"), lax.axis_index("y")
    ctx_index = lax.axis_index("z") * ys + y_index
    positions = ctx_index * block_len + jnp.arange(block_len, dtype=jnp.int32)
    kv_width = KVH * HD
    qkv_width = QD + 2 * kv_width
    scale = HD ** (-0.5)
    share = qkv_weight.shape[0]
    small_share = gains_biases.shape[0]
    ff_share = down_weight.shape[0]
    ff_slab = ff_share * zs * ys
    half = FF // 2
    x_index, z_index = lax.axis_index("x"), lax.axis_index("z")

    small_row = jnp.zeros((1, qkv_width), low).at[0, :small_share].set(gains_biases.astype(low))
    own_attn = jnp.concatenate([qkv_weight.astype(low), out_weight.astype(low)], 1)
    own_attn = jnp.concatenate([own_attn, jnp.pad(small_row, ((0, 0), (0, D)))], 0)
    other = swap("y", own_attn, ys, 1)
    lower = jnp.where(y_index == 0, own_attn, other)
    upper = jnp.where(y_index == 0, other, own_attn)
    pair_out = jnp.concatenate([lower[:share, qkv_width:], upper[:share, qkv_width:]], 0)
    lower, upper = lower[:, :qkv_width], upper[:, :qkv_width]
    spare = jnp.zeros((-2 * (share + 1) % 8, qkv_width), low)
    full_qkv = gather_axis(
        jnp.concatenate([lower[:share], upper[:share], lower[share:], upper[share:], spare], 0),
        "z",
        zs,
    )

    own_gu = (
        gate_up_weight.astype(low)
        .reshape(share, 2, xs, 2, ff_slab)
        .transpose(3, 1, 0, 2, 4)
        .reshape(4, share, half)
    )
    quad = core * 2 + y_index
    quads = place(
        [pick(own_gu, quad)]
        + [swap(("core", "y"), pick(own_gu, quad ^ step), 4, step) for step in range(1, 4)],
        quad,
    ).reshape(2, 2 * share, half)
    quads = jnp.concatenate([quads[0], pair_out, quads[1]], 1)
    quads = [quads] + [swap("z", quads, zs, step) for step in range(1, zs)]
    full_qkv = gather_axis(gather_axis(full_qkv, "x", xs), "core", 2).swapaxes(0, 1)
    full_small = full_qkv[..., 2 * share : 2 * share + ys, :small_share].reshape(-1)
    full_qkv = full_qkv[..., : 2 * share, :].reshape(D, qkv_width)
    full_down = lax.all_gather(down_weight.astype(low), chips, axis=0, tiled=True)

    small_used = full_small.astype(jnp.float32)
    gain_attn = small_used[:D]
    gain_mlp = small_used[D : 2 * D]
    bias = small_used[2 * D :]
    state = inputs.reshape(tokens, D).astype(jnp.float32)
    inverse_attn = lax.rsqrt(jnp.mean(state * state, -1, keepdims=True) + EPS)
    normed = (state * inverse_attn * gain_attn).astype(low)
    qkv = across(full_qkv, normed, 0, 1) + bias[:, None]
    angles = rotation(positions, rows)
    query = (turn(qkv[:QD], angles, 1.0) * scale).astype(low)
    keys = turn(qkv[QD : QD + kv_width], angles, 1.0).astype(low)
    values = qkv[QD + kv_width :].astype(low)
    own_kv = jnp.concatenate(
        [keys.reshape(KVH, HD, tokens), values.reshape(KVH, HD, tokens)], 1
    ).transpose(0, 2, 1)
    own_kv = own_kv.reshape(KVH, rows, block_len, 2 * HD)

    own_kv, quads = hold(own_kv, quads)
    all_kv = gather_axis(own_kv, "z", zs, True)
    first = place([part[:, : half + D] for part in quads], z_index)
    second = place([part[:, half + D :] for part in quads], z_index)
    first = [first] + [swap("x", first, xs, step) for step in range(1, xs)]
    second = [second, swap("y", second, ys, 1)]
    all_kv, first, second = hold(all_kv, first, second)
    all_kv = gather_axis(all_kv, "y", ys)
    first = place(first, x_index)
    first, full_out = first[..., :half], first[..., half:]
    full_out = gather_axis(full_out, "core", 2).swapaxes(0, 1).reshape(QD, D)
    second = place(second, y_index)
    second = [second] + [swap("x", second, xs, step) for step in range(1, xs)]
    all_kv, first = hold(all_kv, first)
    first = [first, swap("y", first, ys, 1)]
    meta = jnp.concatenate([ctx_index.astype(jnp.int32).reshape(1), lengths])
    attended, logs = attention(meta, query, all_kv, block_len)
    attended, first, second = hold(attended, first, second)
    second = place(second, x_index)
    is_gate = y_index == 0
    first = [jnp.where(is_gate, first[0], first[1]), jnp.where(is_gate, first[1], first[0])]
    full_gate = jnp.stack([first[0], second[:, 0]], 1).reshape(D, half)
    full_up = jnp.stack([first[1], second[:, 1]], 1).reshape(D, half)
    mixed_low = attended.astype(low)
    hidden_state = state + across(mixed_low, full_out, 0, 0)
    inverse_mlp = lax.rsqrt(jnp.mean(hidden_state * hidden_state, -1, keepdims=True) + EPS)
    normed2 = (hidden_state * inverse_mlp * gain_mlp).astype(low)
    valid = (positions[None, :] < lengths[:, None]).astype(jnp.float32)
    upstream = cotangent.reshape(tokens, D).astype(jnp.float32) * valid.reshape(tokens, 1)

    def pair(value):
        return jnp.concatenate([value, swap("core", value, 2, 1)], 0)

    def pair_sum(value):
        return value[:tokens] + swap("core", value[tokens:], 2, 1)

    pair_up = pair(upstream.astype(low))
    pair_normed = pair(normed2)
    gate = jnp.dot(pair_normed, full_gate, preferred_element_type=jnp.float32)
    up_part = jnp.dot(pair_normed, full_up, preferred_element_type=jnp.float32)
    sigma = jax.nn.sigmoid(gate)
    activated = gate * sigma
    inner = (activated * up_part).astype(low)
    d_inner = against_weight(pair_up, full_down)
    d_gate = (d_inner * up_part * sigma * (1.0 + gate * (1.0 - sigma))).astype(low)
    d_up = (d_inner * activated).astype(low)
    grad_down = across_tokens(inner, pair_up).astype(low)
    grad_down, d_gate, d_up = hold(grad_down, d_gate, d_up)
    red_down = lax.psum_scatter(grad_down, chips, scatter_dimension=0, tiled=True)
    red_down = red_down.astype(jnp.float32)
    grad_gate = across_tokens(pair_normed, d_gate).astype(low)
    grad_up = across_tokens(pair_normed, d_up).astype(low)
    grad_gate, grad_up, d_gate, d_up = hold(grad_gate, grad_up, d_gate, d_up)
    grad_gate = grad_gate.reshape(xs, 2, zs, 2 * share, half)
    grad_up = grad_up.reshape(xs, 2, zs, 2 * share, half)

    first = [grad_gate[:, 0], grad_up[:, 0]]
    first = [jnp.where(is_gate, first[0], first[1]), jnp.where(is_gate, first[1], first[0])]
    first[1] = swap("y", first[1], ys, 1)
    second = jnp.stack([grad_gate[:, 1], grad_up[:, 1]], 1)
    second = [pick(second, x_index)] + [
        swap("x", pick(second, x_index ^ step), xs, step) for step in range(1, xs)
    ]
    d_normed2 = pair_sum(against_weight(d_gate, full_gate) + against_weight(d_up, full_up))
    output = hidden_state + pair_sum(jnp.dot(inner, full_down, preferred_element_type=jnp.float32))

    change_mlp, grad_gain_mlp = norm_back(hidden_state, inverse_mlp, gain_mlp, d_normed2)
    d_hidden = upstream + change_mlp
    d_hidden_low = d_hidden.astype(low)
    grad_out = across(mixed_low, d_hidden_low, 1, 0)
    d_mixed = across(full_out, d_hidden_low, 1, 1).astype(low)
    grad_out = grad_out.astype(low).reshape(xs, 2, zs, 2 * share, D)
    grad_out = reduce_axis(grad_out, "core", 1, 2).astype(low)

    d_query, kv_terms = [None] * KVH, [None] * KVH
    d_query[0], kv_terms[0] = attention_back(
        0, meta, query, d_mixed, attended, logs, all_kv, block_len
    )
    first, second, d_query[0] = hold(first, second, d_query[0])
    first, second = add_up(first), add_up(second)
    first = jnp.concatenate([first, grad_out], -1)
    kv_terms[0] = reduce_axis(kv_terms[0], "y", 0, ys).astype(low)
    first, second, query = hold(first, second, query)
    first = [pick(first, x_index)] + [
        swap("x", pick(first, x_index ^ step), xs, step) for step in range(1, xs)
    ]
    second = [pick(second, y_index), swap("y", pick(second, 1 - y_index), ys, 1)]
    d_query[1], kv_terms[1] = attention_back(
        1, meta, query, d_mixed, attended, logs, all_kv, block_len
    )
    first, second, d_query[1] = hold(first, second, d_query[1])
    first, second = add_up(first), add_up(second)
    kv_terms[1] = reduce_axis(kv_terms[1], "y", 0, ys).astype(low)
    kv_grads = reduce_axis(jnp.stack(kv_terms, 1), "z", 0, zs, True)
    d_query = jnp.concatenate(d_query, 0)
    red_quads = reduce_axis(jnp.concatenate([first, second], -1), "z", 0, zs).astype(low)
    red_out = red_quads[:, half : half + D]
    red_quads = jnp.stack([red_quads[:, :half], red_quads[:, half + D :]], 0)
    red_quads = red_quads.reshape(4, share, half)
    kv_grads = kv_grads.reshape(KVH, tokens, 2 * HD).transpose(0, 2, 1)
    d_qkv = jnp.concatenate(
        [
            turn(d_query * scale, angles, -1.0),
            turn(kv_grads[:, :HD].reshape(kv_width, tokens), angles, -1.0),
            kv_grads[:, HD:].reshape(kv_width, tokens),
        ],
        0,
    ).astype(low)
    grad_bias = jnp.sum(d_qkv.astype(jnp.float32), 1)
    grad_qkv = across(normed, d_qkv, 0, 1)
    d_normed = across(d_qkv, full_qkv, 0, 1)
    change_attn, grad_gain_attn = norm_back(state, inverse_attn, gain_attn, d_normed)
    input_grad = (d_hidden + change_attn).astype(low)
    grad_small = jnp.concatenate([grad_gain_attn, grad_gain_mlp, grad_bias])

    grad_small = grad_small.astype(low).reshape(-1, ys, small_share)
    grad_small = jnp.pad(grad_small, ((0, 0), (0, 8 - ys), (0, qkv_width - small_share)))
    grad_qkv = jnp.concatenate(
        [grad_qkv.astype(low).reshape(-1, ys * share, qkv_width), grad_small], 1
    )
    red_qkv = to_owners(grad_qkv, sizes)

    red_small = red_qkv[ys * share : ys * share + ys]
    red_qkv = red_qkv[: ys * share].reshape(ys, share, qkv_width)
    red_out = red_out.reshape(ys, share, D)
    along = jnp.zeros((ys, -share % 8, qkv_width + D), low)
    along = along.at[:, 0, :qkv_width].set(red_small)
    along = jnp.concatenate([jnp.concatenate([red_qkv, red_out], 2), along], 1)
    mine = pick(along, y_index).astype(jnp.float32)
    mine = mine + swap("y", pick(along, 1 - y_index), ys, 1).astype(jnp.float32)
    red_qkv, red_out = mine[:share, :qkv_width], mine[:share, qkv_width:]
    red_small = mine[share, :small_share]
    red_gu = place(
        [pick(red_quads, quad)]
        + [swap(("core", "y"), pick(red_quads, quad ^ step), 4, step) for step in range(1, 4)],
        quad,
    )
    red_gu = (
        red_gu.reshape(2, 2, share, xs, ff_slab).transpose(2, 1, 3, 0, 4).reshape(share, 2 * FF)
    ).astype(jnp.float32)

    local_square = (
        jnp.sum(red_qkv * red_qkv)
        + jnp.sum(red_out * red_out)
        + jnp.sum(red_gu * red_gu)
        + jnp.sum(red_down * red_down)
        + jnp.sum(red_small * red_small)
    ).reshape(1)
    square_sum = tree_sum(local_square, "core", 2)
    square_sum = tree_sum(square_sum, ("x", "y"), xs * ys)
    square_sum = tree_sum(square_sum, "z", zs)[0]
    grad_norm = jnp.sqrt(square_sum)
    factor = CLIP / jnp.maximum(grad_norm, CLIP)
    qkv_new = adam_step(red_qkv, qkv_moment, qkv_square, qkv_weight, factor, RATES[0], DECAYS[0])
    out_new = adam_step(red_out, out_moment, out_square, out_weight, factor, RATES[1], DECAYS[1])
    gu_new = adam_step(
        red_gu, gate_up_moment, gate_up_square, gate_up_weight, factor, RATES[2], DECAYS[2]
    )
    down_new = adam_step(
        red_down, down_moment, down_square, down_weight, factor, RATES[3], DECAYS[3]
    )
    small_new = adam_step(
        red_small, small_moment, small_square, gains_biases, factor, RATES[4], DECAYS[4]
    )
    return (
        output.astype(low).reshape(inputs.shape),
        input_grad.reshape(inputs.shape),
        grad_norm,
        *qkv_new,
        *out_new,
        *gu_new,
        *down_new,
        *small_new,
    )


def solution(mesh):
    dp, ctx = mesh.shape["dp"], mesh.shape["ctx"]
    sizes = (dp // 2, ctx // 2, 2)
    fine = Mesh(mesh.devices.reshape(dp // 2, 2, ctx // 2, 2), ("x", "core", "z", "y"))
    seqs, blocks = ("x", "core"), ("z", "y")
    token = P(seqs, blocks, None)
    matrix = P(seqs + blocks, None)
    vector = P(seqs + blocks)
    weights = (matrix,) * 4 + (vector,)
    states = (matrix,) * 8 + (vector,) * 2
    return jax.shard_map(
        functools.partial(layer, sizes),
        mesh=fine,
        in_specs=(token, token, P(seqs)) + weights + states,
        out_specs=(token, token, P()) + (matrix,) * 16 + (vector,) * 4,
        check_vma=False,
    )
```

```python
import functools
import math

import jax
import jax.numpy as jnp
from jax import lax
from jax.experimental import pallas as pl
from jax.experimental.pallas import tpu as pltpu
from jax.sharding import Mesh
from jax.sharding import PartitionSpec as P

D = 896
HEADS = 14
KVH = 2
HD = 64
FF = 4864
STEP = 5
QD = 896


EPS = 1e-06
NEG = -1e30
BASE = 1000000.0
CLIP = 1.0
BETA_ONE = 0.9
BETA_TWO = 0.95
ADAM_EPS = 1e-08
RATES = (0.06, 1.0, 0.06, 0.03, 3.0)
DECAYS = (0.1, 0.1, 0.1, 0.1, 0.0)


def norm_back(state, inverse, gain, upstream):
    scaled = gain * upstream
    change = inverse * scaled - state * inverse**3 * jnp.mean(scaled * state, -1, keepdims=True)
    gain_grad = jnp.sum((upstream * state * inverse).reshape(-1, state.shape[-1]), 0)
    return (change, gain_grad)


def adam_step(gradient, moment, square, weight, factor, rate, decay):
    gradient = gradient * factor
    moment = BETA_ONE * moment + (1.0 - BETA_ONE) * gradient
    square = BETA_TWO * square + (1.0 - BETA_TWO) * gradient * gradient
    corr_one = 1.0 - BETA_ONE**STEP
    corr_two = 1.0 - BETA_TWO**STEP
    update = moment / corr_one / (jnp.sqrt(square / corr_two) + ADAM_EPS)
    weight = weight * (1.0 - rate * decay) - rate * update
    return (gradient, moment, square, weight)


def swap(axis, value, count, step):
    return lax.ppermute(value, axis, [(i, i ^ step) for i in range(count)])


def pick(array, index, dim=0):
    return lax.dynamic_index_in_dim(array, index, dim, keepdims=False)


def place(pieces, index):
    count = range(len(pieces))
    index = index.astype(jnp.int32)
    if len(pieces) == 2:
        index = index > 0
    return jnp.stack([lax.select_n(index, *[pieces[i ^ k] for k in count]) for i in count], 0)


def place_steps(pieces, index):
    out = jnp.zeros((len(pieces),) + pieces[0].shape, pieces[0].dtype)
    for step, piece in enumerate(pieces):
        out = lax.dynamic_update_index_in_dim(out, piece, index ^ step, 0)
    return out


def pieces_along(axis, value, count, up_only=False):
    pieces = [value]
    for step in range(1, count):
        routes = [(i, i ^ step) for i in range(count) if i < i ^ step or not up_only]
        pieces.append(lax.ppermute(value, axis, routes))
    return pieces


def gather_axis(value, axis, count):
    return place(pieces_along(axis, value, count), lax.axis_index(axis))


def total_of(parts):
    total = parts[0].astype(jnp.float32)
    for part in parts[1:]:
        total = total + part.astype(jnp.float32)
    return total


def add_up(parts):
    return total_of(parts).astype(jnp.bfloat16)


def parts_along(axis, array, dim, count, down_only=False):
    index = lax.axis_index(axis)
    parts = [pick(array, index, dim)]
    for step in range(1, count):
        routes = [(i, i ^ step) for i in range(count) if i ^ step < i or not down_only]
        parts.append(lax.ppermute(pick(array, index ^ step, dim), axis, routes))
    return parts


def reduce_axis(array, axis, dim, count):
    return total_of(parts_along(axis, array, dim, count))


def hold(*values):
    return lax.optimization_barrier(values)


def tree_sum(value, axis, count):
    step = 1
    while step < count:
        value = value + swap(axis, value, count, step)
        step *= 2
    return value


def across(left, right, left_dim, right_dim):
    return lax.dot_general(
        left, right, (((left_dim,), (right_dim,)), ((), ())), preferred_element_type=jnp.float32
    )


def rotation(positions, rows):
    half = HD // 2
    freq = jnp.exp(jnp.arange(half, dtype=jnp.float32) * (-2.0 * math.log(BASE) / HD))
    angle = jnp.tile(freq[:, None] * positions.astype(jnp.float32)[None, :], (1, rows))
    return (jnp.cos(angle), jnp.sin(angle))


def turn(tensor, angles, sign):
    cosine, sine = angles[0], sign * angles[1]
    first, second = jnp.split(tensor.reshape(-1, 2, HD // 2, tensor.shape[-1]), 2, 1)
    return jnp.concatenate(
        [first * cosine - second * sine, second * cosine + first * sine], 1
    ).reshape(tensor.shape)


def attend_kernel(group, block, meta, q_ref, kv_ref, out_ref, log_ref, top, total, accum):
    ctx, length = meta[0], meta[1 + pl.program_id(1)]
    blocks_y = kv_ref.shape[0]
    top[...] = jnp.full(top.shape, NEG, jnp.float32)
    total[...] = jnp.zeros(total.shape, jnp.float32)
    accum[...] = jnp.zeros(accum.shape, jnp.float32)

    def step(index, masked):
        pair = kv_ref[index % blocks_y, index // blocks_y, 0, 0]
        keys = pair[:, :HD]
        values = pair.T[HD:]
        if masked:
            key_pos = index * block + lax.broadcasted_iota(jnp.int32, (block, block), 0)
            query_pos = ctx * block + lax.broadcasted_iota(jnp.int32, (block, block), 1)
            allowed = (key_pos <= query_pos) & (key_pos < length)
        heads = range(group)
        span = [slice(head * HD, (head + 1) * HD) for head in heads]
        scores = [
            jnp.dot(keys, q_ref[span[head]], preferred_element_type=jnp.float32) for head in heads
        ]
        if masked:
            scores = [jnp.where(allowed, part, NEG) for part in scores]
        old = top[...]
        new = jnp.maximum(
            old, jnp.concatenate([jnp.max(part, 0, keepdims=True) for part in scores], 0)
        )
        factor = jnp.exp(old - new)
        top[...] = new
        probs = [jnp.exp(scores[head] - new[head : head + 1]) for head in heads]
        total[...] = total[...] * factor + jnp.concatenate(
            [jnp.sum(part, 0, keepdims=True) for part in probs], 0
        )
        weighted = [
            jnp.dot(values, part.astype(jnp.bfloat16), preferred_element_type=jnp.float32)
            for part in probs
        ]
        for head in heads:
            accum[span[head]] = accum[span[head]] * factor[head : head + 1] + weighted[head]

    clear = jnp.minimum(ctx, length // block)
    last = jnp.minimum(ctx + 1, (length + block - 1) // block)
    pl.loop(0, clear)(lambda index: step(index, False))
    pl.loop(clear, last)(lambda index: step(index, True))
    for head in range(group):
        rows = slice(head * HD, (head + 1) * HD)
        out_ref[rows] = accum[rows] / total[head : head + 1]
    log_ref[0] = top[...] + jnp.log(total[...])


def attend_back_kernel(
    group, block, meta, q_ref, g_ref, out_ref, log_ref, kv_ref, dq_ref, dkv_ref, both, delta
):
    ctx, length = meta[0], meta[1 + pl.program_id(0)]
    blocks_y, blocks_z = kv_ref.shape[0], kv_ref.shape[1]
    dq_ref[...] = jnp.zeros(dq_ref.shape, jnp.float32)
    for head in range(group):
        rows = slice(head * HD, (head + 1) * HD)
        query, upper = q_ref[rows], g_ref[rows]
        both[head] = jnp.concatenate([query, upper], 0).T
        delta[head : head + 1] = jnp.sum(upper.astype(jnp.float32) * out_ref[rows], 0, keepdims=True)
    lane = lax.broadcasted_iota(jnp.int32, (block, 2 * HD), 1)

    def step(index, masked):
        pair = kv_ref[index % blocks_y, index // blocks_y, 0, 0]
        keys, values = pair[:, :HD], pair[:, HD:]
        keys_across = pair.T[:HD]
        if masked:
            key_pos = index * block + lax.broadcasted_iota(jnp.int32, (block, block), 0)
            query_pos = ctx * block + lax.broadcasted_iota(jnp.int32, (block, block), 1)
            allowed = (key_pos <= query_pos) & (key_pos < length)
        d_keys = jnp.zeros((block, 2 * HD), jnp.float32)
        d_values = jnp.zeros((block, 2 * HD), jnp.float32)
        heads = range(group)
        span = [slice(head * HD, (head + 1) * HD) for head in heads]
        scores = [
            jnp.dot(keys, q_ref[span[head]], preferred_element_type=jnp.float32) for head in heads
        ]
        d_probs = [
            jnp.dot(values, g_ref[span[head]], preferred_element_type=jnp.float32) for head in heads
        ]
        probs = [jnp.exp(scores[head] - log_ref[0, head : head + 1]) for head in heads]
        if masked:
            probs = [jnp.where(allowed, part, 0.0) for part in probs]
        d_scores = [
            (probs[head] * (d_probs[head] - delta[head : head + 1])).astype(jnp.bfloat16)
            for head in heads
        ]
        probs = [part.astype(jnp.bfloat16) for part in probs]
        d_query = [
            jnp.dot(keys_across, part, preferred_element_type=jnp.float32) for part in d_scores
        ]
        for head in heads:
            d_keys += jnp.dot(d_scores[head], both[head], preferred_element_type=jnp.float32)
        for head in heads:
            d_values += jnp.dot(probs[head], both[head], preferred_element_type=jnp.float32)
        for head in heads:
            dq_ref[span[head]] += d_query[head]
        merged = jnp.where(lane < HD, d_keys, d_values)
        dkv_ref[index % blocks_y, index // blocks_y, 0] = merged.astype(jnp.bfloat16)

    clear = jnp.minimum(ctx, length // block)
    last = jnp.minimum(ctx + 1, (length + block - 1) // block)
    pl.loop(0, clear)(lambda index: step(index, False))
    pl.loop(clear, last)(lambda index: step(index, True))

    @pl.loop(last, blocks_y * blocks_z)
    def _(index):
        dkv_ref[index % blocks_y, index // blocks_y, 0] = jnp.zeros(
            (block, 2 * HD), jnp.bfloat16
        )


def attention(meta, query, all_kv, block):
    ys, zs, _, rows, _, _ = all_kv.shape
    group = HEADS // KVH
    wide = pl.BlockSpec((group * HD, block), lambda h, r, meta: (h, r))
    pairs = pl.BlockSpec((ys, zs, 1, 1, block, 2 * HD), lambda h, r, meta: (0, 0, h, r, 0, 0))
    logs = pl.BlockSpec((1, group, block), lambda h, r, meta: (h, 0, r))
    return pl.pallas_call(
        functools.partial(attend_kernel, group, block),
        grid_spec=pltpu.PrefetchScalarGridSpec(
            num_scalar_prefetch=1,
            grid=(KVH, rows),
            in_specs=[wide, pairs],
            out_specs=[wide, logs],
            scratch_shapes=[
                pltpu.VMEM((group, block), jnp.float32),
                pltpu.VMEM((group, block), jnp.float32),
                pltpu.VMEM((group * HD, block), jnp.float32),
            ],
        ),
        out_shape=[
            jax.ShapeDtypeStruct((QD, rows * block), jnp.float32),
            jax.ShapeDtypeStruct((KVH, group, rows * block), jnp.float32),
        ],
        compiler_params=pltpu.CompilerParams(vmem_limit_bytes=32 * 2**20),
        cost_estimate=pl.CostEstimate(flops=1, bytes_accessed=1, transcendentals=0),
        name="attend",
    )(meta, query, all_kv)


def attention_back(h, meta, query, upper, attended, logs, all_kv, block):
    ys, zs, _, rows, _, _ = all_kv.shape
    group = HEADS // KVH
    wide = pl.BlockSpec((group * HD, block), lambda r, meta: (h, r))
    narrow = pl.BlockSpec((group * HD, block), lambda r, meta: (0, r))
    pairs = pl.BlockSpec((ys, zs, 1, 1, block, 2 * HD), lambda r, meta: (0, 0, h, r, 0, 0))
    terms = pl.BlockSpec((ys, zs, 1, block, 2 * HD), lambda r, meta: (0, 0, r, 0, 0))
    log_spec = pl.BlockSpec((1, group, block), lambda r, meta: (h, 0, r))
    return pl.pallas_call(
        functools.partial(attend_back_kernel, group, block),
        grid_spec=pltpu.PrefetchScalarGridSpec(
            num_scalar_prefetch=1,
            grid=(rows,),
            in_specs=[wide, wide, wide, log_spec, pairs],
            out_specs=[narrow, terms],
            scratch_shapes=[
                pltpu.VMEM((group, block, 2 * HD), jnp.bfloat16),
                pltpu.VMEM((group, block), jnp.float32),
            ],
        ),
        out_shape=[
            jax.ShapeDtypeStruct((group * HD, rows * block), jnp.float32),
            jax.ShapeDtypeStruct((ys, zs, rows, block, 2 * HD), jnp.bfloat16),
        ],
        compiler_params=pltpu.CompilerParams(vmem_limit_bytes=32 * 2**20),
        cost_estimate=pl.CostEstimate(flops=1, bytes_accessed=1, transcendentals=0),
        name="attend_back",
    )(meta, query, upper, attended, logs, all_kv)


def dot(left, right, left_dim=1, right_dim=0):
    return lax.dot_general(
        left, right, (((left_dim,), (right_dim,)), ((), ())), preferred_element_type=jnp.float32
    )


def hidden_kernel(xs, chunk, spot, n_own, n_other, u_own, u_other, first_a, first_b, *refs):
    seconds, (down_ref, inner_ref, d_ref, gate_ref, up_ref, across_ref) = refs[:xs], refs[xs:]
    y, x = spot[0], spot[1]
    count = n_own.shape[0]

    swapped = y != 0
    lower = [jnp.where(swapped, first_b[...], first_a[...]), jnp.where(swapped, first_a[...], first_b[...])]
    size = first_a.shape[1]
    for index, out in enumerate((gate_ref, up_ref)):
        for i in range(xs):
            out[2 * i * size : (2 * i + 1) * size] = lower[index][i]
            upper = seconds[i][index]
            for other in range(xs):
                if other != i:
                    upper = jnp.where((x ^ i) == other, seconds[other][index], upper)
            out[(2 * i + 1) * size : (2 * i + 2) * size] = upper

    @pl.when(pl.program_id(0) == 0)
    def _():
        for ref, columns in ((n_own, slice(0, count)), (n_other, slice(count, 2 * count))):
            turned = ref[...].T
            for i in range(xs):
                across_ref[i, :, columns] = turned[2 * i * size : (2 * i + 1) * size]
                across_ref[xs + (x ^ i), :, columns] = turned[(2 * i + 1) * size : (2 * i + 2) * size]

    gate_w, up_w, down_w = gate_ref[...], up_ref[...], down_ref[...]
    spans = [slice(i, i + chunk) for i in range(0, count, chunk)]
    gates = [dot(ref[span], gate_w) for ref in (n_own, n_other) for span in spans]
    ups = [dot(ref[span], up_w) for ref in (n_own, n_other) for span in spans]
    inners = [dot(ref[span], down_w, 1, 1) for ref in (u_own, u_other) for span in spans]
    parts = [slice(i, i + chunk) for i in range(0, 2 * count, chunk)]
    for part, gate, up, d_inner in zip(parts, gates, ups, inners):
        sigma = 1.0 / (1.0 + jnp.exp(-gate))
        activated = gate * sigma
        inner_ref[part] = (activated * up).astype(jnp.bfloat16)
        d_ref[1, part] = (d_inner * activated).astype(jnp.bfloat16)
        d_ref[0, part] = (d_inner * up * (sigma + activated * (1.0 - sigma))).astype(jnp.bfloat16)


def hidden_part(spot, normed, upper, first, second, down, width=256):
    count, size = normed[0].shape
    half = down.shape[0]
    xs, slab, _ = first[0].shape
    whole = pl.BlockSpec((count, size), lambda i, spot: (0, 0))
    lower = pl.BlockSpec((xs, slab, width), lambda i, spot: (0, 0, i))
    both = pl.BlockSpec((2, slab, width), lambda i, spot: (0, 0, i))
    columns = pl.BlockSpec((size, width), lambda i, spot: (0, i))
    rows = pl.BlockSpec((width, size), lambda i, spot: (i, 0))
    shapes = [(2 * count, half), (2, 2 * count, half), (size, half), (size, half)]
    shapes += [(2 * xs, slab, 2 * count)]
    return pl.pallas_call(
        functools.partial(hidden_kernel, xs, 256),
        grid_spec=pltpu.PrefetchScalarGridSpec(
            num_scalar_prefetch=1,
            grid=(pl.cdiv(half, width),),
            in_specs=[whole] * 4 + [lower] * 2 + [both] * xs + [rows],
            out_specs=[
                pl.BlockSpec((2 * count, width), lambda i, spot: (0, i)),
                pl.BlockSpec((2, 2 * count, width), lambda i, spot: (0, 0, i)),
                columns,
                columns,
                pl.BlockSpec((2 * xs, slab, 2 * count), lambda i, spot: (0, 0, 0)),
            ],
        ),
        out_shape=[jax.ShapeDtypeStruct(shape, jnp.bfloat16) for shape in shapes],
        compiler_params=pltpu.CompilerParams(vmem_limit_bytes=56 * 2**20),
        cost_estimate=pl.CostEstimate(flops=1, bytes_accessed=1, transcendentals=0),
        name="hidden",
    )(spot, *normed, *upper, *first, *second, down)


def grads_kernel(xs, spot, n_ref, d_own, d_other, *outs):
    y = spot[0]
    rows = n_ref.shape[1]
    features = n_ref[...].reshape(-1, n_ref.shape[2])
    for out, index, ref in zip(outs[:2], (y, 1 - y), (d_own, d_other)):
        result = dot(features, ref[...]).astype(jnp.bfloat16)
        out[...] = result[: xs * rows].reshape(out.shape)
        for step, upper in enumerate(outs[2:]):
            upper[index] = result[(xs + step) * rows : (xs + step + 1) * rows]


def gate_up_grads(spot, features, d_both, xs, start, stop, width):
    _, rows, count = features.shape
    first = start // width
    lower = pl.BlockSpec((xs, rows, width), lambda i, spot: (0, 0, i))
    upper = pl.BlockSpec((2, rows, width), lambda i, spot: (0, 0, i))
    return pl.pallas_call(
        functools.partial(grads_kernel, xs),
        grid_spec=pltpu.PrefetchScalarGridSpec(
            num_scalar_prefetch=1,
            grid=(pl.cdiv(stop - start, width),),
            in_specs=[
                pl.BlockSpec((2 * xs, rows, count), lambda i, spot: (0, 0, 0)),
                pl.BlockSpec((None, count, width), lambda i, spot: (spot[0], 0, first + i)),
                pl.BlockSpec((None, count, width), lambda i, spot: (1 - spot[0], 0, first + i)),
            ],
            out_specs=[lower] * 2 + [upper] * xs,
        ),
        out_shape=[jax.ShapeDtypeStruct((xs, rows, stop - start), jnp.bfloat16)] * 2
        + [jax.ShapeDtypeStruct((2, rows, stop - start), jnp.bfloat16)] * xs,
        compiler_params=pltpu.CompilerParams(vmem_limit_bytes=56 * 2**20),
        cost_estimate=pl.CostEstimate(flops=1, bytes_accessed=1, transcendentals=0),
        name="gate_up_grads",
    )(spot, features, d_both, d_both)


def down_kernel(inner_ref, u_own, u_other, out_ref):
    count = u_own.shape[0]
    result = dot(inner_ref[:count], u_own[...], 0, 0) + dot(inner_ref[count:], u_other[...], 0, 0)
    out_ref[...] = result.astype(jnp.bfloat16)


def down_grad(inner, upper, width=256):
    count, half = inner.shape
    size = upper[0].shape[1]
    return pl.pallas_call(
        down_kernel,
        grid=(pl.cdiv(half, width),),
        in_specs=[
            pl.BlockSpec((count, width), lambda i: (0, i)),
            pl.BlockSpec((count // 2, size), lambda i: (0, 0)),
            pl.BlockSpec((count // 2, size), lambda i: (0, 0)),
        ],
        out_specs=pl.BlockSpec((width, size), lambda i: (i, 0)),
        out_shape=jax.ShapeDtypeStruct((half, size), jnp.bfloat16),
        compiler_params=pltpu.CompilerParams(vmem_limit_bytes=56 * 2**20),
        cost_estimate=pl.CostEstimate(flops=1, bytes_accessed=1, transcendentals=0),
        name="down_grad",
    )(inner, *upper)


def back_kernel(steps, d_ref, gate_ref, up_ref, own_ref, other_ref):
    result = dot(d_ref[0], gate_ref[...], 1, 1) + dot(d_ref[1], up_ref[...], 1, 1)

    @pl.when(pl.program_id(0) < steps)
    def _():
        own_ref[...] = result

    @pl.when(pl.program_id(0) >= steps)
    def _():
        other_ref[...] = result


def hidden_back(d_both, gate, up, height=256):
    _, count, half = d_both.shape
    size = gate.shape[0]
    steps = count // height // 2
    whole = pl.BlockSpec((size, half), lambda i: (0, 0))
    return pl.pallas_call(
        functools.partial(back_kernel, steps),
        grid=(2 * steps,),
        in_specs=[pl.BlockSpec((2, height, half), lambda i: (0, i, 0)), whole, whole],
        out_specs=[
            pl.BlockSpec((height, size), lambda i: (jnp.minimum(i, steps - 1), 0)),
            pl.BlockSpec((height, size), lambda i: (jnp.maximum(i, steps) - steps, 0)),
        ],
        out_shape=[jax.ShapeDtypeStruct((count // 2, size), jnp.float32)] * 2,
        compiler_params=pltpu.CompilerParams(vmem_limit_bytes=56 * 2**20),
        cost_estimate=pl.CostEstimate(flops=1, bytes_accessed=1, transcendentals=0),
        name="hidden_back",
    )(d_both, gate, up)


def layer(
    sizes,
    inputs,
    cotangent,
    lengths,
    qkv_weight,
    out_weight,
    gate_up_weight,
    down_weight,
    gains_biases,
    qkv_moment,
    qkv_square,
    out_moment,
    out_square,
    gate_up_moment,
    gate_up_square,
    down_moment,
    down_square,
    small_moment,
    small_square,
):
    xs, zs, ys = sizes
    everyone = ("x", "core", "z", "y")
    chips = ("x", "z", "y")
    low = jnp.bfloat16
    rows, block_len, width = inputs.shape
    tokens = rows * block_len
    core, y_index = lax.axis_index("core"), lax.axis_index("y")
    ctx_index = lax.axis_index("z") * ys + y_index
    positions = ctx_index * block_len + jnp.arange(block_len, dtype=jnp.int32)
    kv_width = KVH * HD
    qkv_width = QD + 2 * kv_width
    scale = HD ** (-0.5)
    share = qkv_weight.shape[0]
    small_share = gains_biases.shape[0]
    ff_share = down_weight.shape[0]
    ff_slab = ff_share * zs * ys
    half = FF // 2
    x_index, z_index = lax.axis_index("x"), lax.axis_index("z")

    small_row = jnp.zeros((1, qkv_width), low).at[0, :small_share].set(gains_biases.astype(low))
    own_attn = jnp.concatenate([qkv_weight.astype(low), out_weight.astype(low)], 1)
    own_attn = jnp.concatenate([own_attn, jnp.pad(small_row, ((0, 0), (0, D)))], 0)
    other = swap("y", own_attn, ys, 1)
    lower = jnp.where(y_index == 0, own_attn, other)
    upper = jnp.where(y_index == 0, other, own_attn)
    pair_out = jnp.concatenate([lower[:share, qkv_width:], upper[:share, qkv_width:]], 0)
    lower, upper = lower[:, :qkv_width], upper[:, :qkv_width]
    spare = jnp.zeros((-2 * (share + 1) % 8, qkv_width), low)
    full_qkv = pieces_along(
        "z",
        jnp.concatenate([lower[:share], upper[:share], lower[share:], upper[share:], spare], 0),
        zs,
    )

    own_gu = (
        gate_up_weight.astype(low)
        .reshape(share, 2, xs, 2, ff_slab)
        .transpose(3, 1, 0, 2, 4)
        .reshape(4, share, half)
    )
    quad = core * 2 + y_index
    quads = place(
        [pick(own_gu, quad)]
        + [swap(("core", "y"), pick(own_gu, quad ^ step), 4, step) for step in range(1, 4)],
        quad,
    ).reshape(2, 2 * share, half)
    first = jnp.concatenate([quads[0], pair_out], 1)
    full_qkv, first, second = hold(full_qkv, first, quads[1])
    first = pieces_along("z", first, zs)
    full_qkv = pieces_along("x", place_steps(full_qkv, z_index), xs)
    full_qkv, first, second = hold(full_qkv, first, second)
    second = pieces_along("z", second, zs)
    first = pieces_along("x", place(first, z_index), xs)
    full_qkv = gather_axis(place(full_qkv, x_index), "core", 2).swapaxes(0, 1)
    full_small = full_qkv[..., 2 * share : 2 * share + ys, :small_share].reshape(-1)
    full_qkv = full_qkv[..., : 2 * share, :].reshape(D, qkv_width)

    small_used = full_small.astype(jnp.float32)
    gain_attn = small_used[:D]
    gain_mlp = small_used[D : 2 * D]
    bias = small_used[2 * D :]
    state = inputs.reshape(tokens, D).astype(jnp.float32)
    inverse_attn = lax.rsqrt(jnp.mean(state * state, -1, keepdims=True) + EPS)
    normed = (state * inverse_attn * gain_attn).astype(low)
    qkv = across(full_qkv, normed, 0, 1) + bias[:, None]
    angles = rotation(positions, rows)
    query = (turn(qkv[:QD], angles, 1.0) * scale).astype(low)
    keys = turn(qkv[QD : QD + kv_width], angles, 1.0).astype(low)
    values = qkv[QD + kv_width :].astype(low)
    own_kv = jnp.concatenate(
        [keys.reshape(KVH, HD, tokens), values.reshape(KVH, HD, tokens)], 1
    ).transpose(0, 2, 1)
    own_kv = own_kv.reshape(KVH, rows, block_len, 2 * HD)

    valid = (positions[None, :] < lengths[:, None]).astype(jnp.float32)
    upstream = cotangent.reshape(tokens, D).astype(jnp.float32) * valid.reshape(tokens, 1)

    own_kv, second, down_weight, upstream = hold(own_kv, second, down_weight, upstream)
    full_down = lax.all_gather(down_weight.astype(low), chips, axis=0, tiled=True)
    all_kv = pieces_along("z", own_kv, zs, True)
    second = pieces_along("y", place(second, z_index), ys)
    all_kv, first, second, upstream = hold(all_kv, first, second, upstream)
    all_kv = pieces_along("y", place(all_kv, z_index), ys)
    second = pieces_along("x", place(second, y_index), xs)
    first = place(first, x_index)
    first, full_out = first[..., :half], first[..., half:]
    all_kv, first, full_out, upstream = hold(all_kv, first, full_out, upstream)
    all_kv = place(all_kv, y_index)
    full_out = gather_axis(full_out, "core", 2).swapaxes(0, 1).reshape(QD, D)
    first = pieces_along("y", first, ys)
    meta = jnp.concatenate([ctx_index.astype(jnp.int32).reshape(1), lengths])
    attended, logs = attention(meta, query, all_kv, block_len)
    attended, first, second = hold(attended, first, second)
    spot = jnp.stack([y_index, x_index]).astype(jnp.int32)
    slab = D // (2 * xs)
    first = [part.reshape(xs, slab, half) for part in first]
    second = [part.reshape(2, slab, half) for part in second]
    mixed_low = attended.astype(low)
    hidden_state = state + across(mixed_low, full_out, 0, 0)
    inverse_mlp = lax.rsqrt(jnp.mean(hidden_state * hidden_state, -1, keepdims=True) + EPS)
    normed2 = (hidden_state * inverse_mlp * gain_mlp).astype(low)

    def pair(value):
        return value, swap("core", value, 2, 1)

    def pair_sum(value):
        return value[:tokens] + swap("core", value[tokens:], 2, 1)

    pair_up = pair(upstream.astype(low))
    pair_normed = pair(normed2)
    inner, d_both, full_gate, full_up, features = hidden_part(
        spot, pair_normed, pair_up, first, second, full_down
    )

    middle = half // 256 // 2 * 256 + 128

    def exchange(parts):
        first, second = list(parts[:2]), list(parts[2:])
        first[1] = swap("y", first[1], ys, 1)
        return first, second[:1] + [swap("x", second[i], xs, i) for i in range(1, xs)]

    cut = ff_share // 16 * 8
    grad_down = down_grad(inner, pair_up, 512)
    grad_down, d_both = hold(grad_down, d_both)
    grad_down = grad_down.reshape(xs, zs, ys, ff_share, D)
    down_y = parts_along("y", grad_down[:, :, :, :cut], 2, ys)
    down_x = parts_along("x", grad_down[:, :, :, cut:], 0, xs)
    left = gate_up_grads(spot, features, d_both, xs, 0, middle, 384)
    right = gate_up_grads(spot, features, d_both, xs, middle, half, 384)
    down_y, down_x, left, right, d_both, inner = hold(down_y, down_x, left, right, d_both, inner)
    left = exchange(left)
    down_y = parts_along("x", add_up(down_y), 0, xs)
    down_x = parts_along("y", add_up(down_x), 1, ys)
    d_normed2 = hidden_back(d_both, full_gate, full_up)
    output = jnp.dot(inner, full_down, preferred_element_type=jnp.float32)
    left, down_y, down_x, right, d_normed2, output = hold(
        left, down_y, down_x, right, d_normed2, output
    )
    right = exchange(right)
    first = parts_along("x", add_up(left[0]), 0, xs)
    second = parts_along("y", add_up(left[1]), 0, ys)
    d_normed2 = d_normed2[0] + swap("core", d_normed2[1], 2, 1)

    change_mlp, grad_gain_mlp = norm_back(hidden_state, inverse_mlp, gain_mlp, d_normed2)
    d_hidden = upstream + change_mlp
    d_hidden_low = d_hidden.astype(low)
    grad_out = across(mixed_low, d_hidden_low, 1, 0)
    d_mixed = across(full_out, d_hidden_low, 1, 1).astype(low)
    grad_out = parts_along(
        "core", grad_out.astype(low).reshape(xs, 2, zs, 2 * share, D), 1, 2
    )
    d_query, kv_terms = [None] * KVH, [None] * KVH
    d_query[0], kv_terms[0] = attention_back(
        0, meta, query, d_mixed, attended, logs, all_kv, block_len
    )
    right, first, second, grad_out, d_query[0], kv_terms[0], query = hold(
        right, first, second, grad_out, d_query[0], kv_terms[0], query
    )
    left = jnp.concatenate([add_up(first), add_up(second)], -1)
    left = parts_along("z", left.reshape(zs, 2 * share, -1), 0, zs)
    first = add_up(right[0]).reshape(xs, zs, 2 * share, -1)
    first = parts_along("x", jnp.concatenate([first, add_up(grad_out)], -1), 0, xs)
    second = parts_along("y", add_up(right[1]), 0, ys)
    d_query[1], kv_terms[1] = attention_back(
        1, meta, query, d_mixed, attended, logs, all_kv, block_len
    )
    left, first, second, kv_terms, d_query[1] = hold(left, first, second, kv_terms, d_query[1])
    kv_terms = parts_along("y", jnp.stack(kv_terms, 2), 0, ys)
    right = jnp.concatenate([add_up(first), add_up(second).reshape(zs, 2 * share, -1)], -1)
    right = parts_along("z", right, 0, zs)
    output = hidden_state + pair_sum(output)
    kv_terms, right, output, left, down_y, down_x = hold(
        kv_terms, right, output, left, down_y, down_x
    )
    kv_terms = parts_along("z", add_up(kv_terms), 0, zs, True)
    left, right = add_up(left), add_up(right)
    red_out = right[:, half - middle : half - middle + D]
    red_quads = jnp.stack(
        [
            jnp.concatenate([left[:, :middle], right[:, : half - middle]], 1),
            jnp.concatenate([left[:, middle:], right[:, half - middle + D :]], 1),
        ],
        0,
    )
    red_quads = parts_along("y", red_quads.reshape(2, ys, share, half), 1, ys)
    red_down = jnp.concatenate([add_up(down_y), add_up(down_x)], 1)
    kv_terms, red_quads, red_down = hold(kv_terms, red_quads, red_down)
    kv_grads = total_of(kv_terms)
    red_down = parts_along("z", red_down, 0, zs)
    red_gu = parts_along("core", place(red_quads, y_index), 1, 2)
    d_query = jnp.concatenate(d_query, 0)
    kv_grads = kv_grads.reshape(KVH, tokens, 2 * HD).transpose(0, 2, 1)
    d_qkv = jnp.concatenate(
        [
            turn(d_query * scale, angles, -1.0),
            turn(kv_grads[:, :HD].reshape(kv_width, tokens), angles, -1.0),
            kv_grads[:, HD:].reshape(kv_width, tokens),
        ],
        0,
    ).astype(low)
    grad_bias = jnp.sum(d_qkv.astype(jnp.float32), 1)
    grad_qkv = across(normed, d_qkv, 0, 1)
    d_normed = across(d_qkv, full_qkv, 0, 1)
    change_attn, grad_gain_attn = norm_back(state, inverse_attn, gain_attn, d_normed)
    input_grad = (d_hidden + change_attn).astype(low)
    grad_small = jnp.concatenate([grad_gain_attn, grad_gain_mlp, grad_bias])

    grad_small = grad_small.astype(low).reshape(-1, ys, small_share)
    grad_small = jnp.pad(grad_small, ((0, 0), (0, 8 - ys), (0, qkv_width - small_share)))
    grad_qkv = jnp.concatenate(
        [grad_qkv.astype(low).reshape(-1, ys * share, qkv_width), grad_small], 1
    )
    red_qkv = grad_qkv.reshape(xs, 2, zs, -1, qkv_width)
    red_qkv = add_up(parts_along("core", red_qkv, 1, 2))
    red_qkv = parts_along("x", red_qkv, 0, xs)
    red_qkv, red_down, red_gu = hold(red_qkv, red_down, red_gu)
    red_qkv = add_up(parts_along("z", add_up(red_qkv), 0, zs))
    red_down = total_of(red_down)

    red_small = red_qkv[ys * share : ys * share + ys]
    red_qkv = red_qkv[: ys * share].reshape(ys, share, qkv_width)
    red_out = red_out.reshape(ys, share, D)
    along = jnp.zeros((ys, -share % 8, qkv_width + D), low)
    along = along.at[:, 0, :qkv_width].set(red_small)
    along = jnp.concatenate([jnp.concatenate([red_qkv, red_out], 2), along], 1)
    mine = pick(along, y_index).astype(jnp.float32)
    mine = mine + swap("y", pick(along, 1 - y_index), ys, 1).astype(jnp.float32)
    red_qkv, red_out = mine[:share, :qkv_width], mine[:share, qkv_width:]
    red_small = mine[share, :small_share]
    red_gu = place(red_gu, core)
    red_gu = (
        red_gu.reshape(2, 2, share, xs, ff_slab).transpose(2, 1, 3, 0, 4).reshape(share, 2 * FF)
    ).astype(jnp.float32)

    local_square = (
        jnp.sum(red_qkv * red_qkv)
        + jnp.sum(red_out * red_out)
        + jnp.sum(red_gu * red_gu)
        + jnp.sum(red_down * red_down)
        + jnp.sum(red_small * red_small)
    ).reshape(1)
    square_sum = local_square
    for axis, count in (("core", 2), ("y", ys), ("x", xs), ("z", zs)):
        square_sum = tree_sum(square_sum, axis, count)
    square_sum = square_sum[0]
    grad_norm = jnp.sqrt(square_sum)
    factor = CLIP / jnp.maximum(grad_norm, CLIP)
    qkv_new = adam_step(red_qkv, qkv_moment, qkv_square, qkv_weight, factor, RATES[0], DECAYS[0])
    out_new = adam_step(red_out, out_moment, out_square, out_weight, factor, RATES[1], DECAYS[1])
    gu_new = adam_step(
        red_gu, gate_up_moment, gate_up_square, gate_up_weight, factor, RATES[2], DECAYS[2]
    )
    down_new = adam_step(
        red_down, down_moment, down_square, down_weight, factor, RATES[3], DECAYS[3]
    )
    small_new = adam_step(
        red_small, small_moment, small_square, gains_biases, factor, RATES[4], DECAYS[4]
    )
    return (
        output.astype(low).reshape(inputs.shape),
        input_grad.reshape(inputs.shape),
        grad_norm,
        *qkv_new,
        *out_new,
        *gu_new,
        *down_new,
        *small_new,
    )


def solution(mesh):
    dp, ctx = mesh.shape["dp"], mesh.shape["ctx"]
    sizes = (dp // 2, ctx // 2, 2)
    fine = Mesh(mesh.devices.reshape(dp // 2, 2, ctx // 2, 2), ("x", "core", "z", "y"))
    seqs, blocks = ("x", "core"), ("z", "y")
    token = P(seqs, blocks, None)
    matrix = P(seqs + blocks, None)
    vector = P(seqs + blocks)
    weights = (matrix,) * 4 + (vector,)
    states = (matrix,) * 8 + (vector,) * 2
    return jax.shard_map(
        functools.partial(layer, sizes),
        mesh=fine,
        in_specs=(token, token, P(seqs)) + weights + states,
        out_specs=(token, token, P()) + (matrix,) * 16 + (vector,) * 4,
        check_vma=False,
    )
```

```python
import functools
import math

import jax
import jax.numpy as jnp
from jax import lax
from jax.experimental import pallas as pl
from jax.experimental.pallas import tpu as pltpu
from jax.sharding import Mesh
from jax.sharding import PartitionSpec as P

D = 896
HEADS = 14
KVH = 2
HD = 64
FF = 4864
STEP = 5
QD = 896


EPS = 1e-06
NEG = -1e30
BASE = 1000000.0
CLIP = 1.0
BETA_ONE = 0.9
BETA_TWO = 0.95
ADAM_EPS = 1e-08
RATES = (0.06, 1.0, 0.06, 0.03, 3.0)
DECAYS = (0.1, 0.1, 0.1, 0.1, 0.0)


def norm_back(state, inverse, gain, upstream):
    scaled = gain * upstream
    change = inverse * scaled - state * inverse**3 * jnp.mean(scaled * state, -1, keepdims=True)
    gain_grad = jnp.sum((upstream * state * inverse).reshape(-1, state.shape[-1]), 0)
    return (change, gain_grad)


def adam_step(gradient, moment, square, weight, factor, rate, decay):
    gradient = gradient * factor
    moment = BETA_ONE * moment + (1.0 - BETA_ONE) * gradient
    square = BETA_TWO * square + (1.0 - BETA_TWO) * gradient * gradient
    corr_one = 1.0 - BETA_ONE**STEP
    corr_two = 1.0 - BETA_TWO**STEP
    update = moment / corr_one / (jnp.sqrt(square / corr_two) + ADAM_EPS)
    weight = weight * (1.0 - rate * decay) - rate * update
    return (gradient, moment, square, weight)


def swap(axis, value, count, step):
    return lax.ppermute(value, axis, [(i, i ^ step) for i in range(count)])


def pick(array, index, dim=0):
    return lax.dynamic_index_in_dim(array, index, dim, keepdims=False)


def place(pieces, index):
    count = range(len(pieces))
    index = index.astype(jnp.int32)
    if len(pieces) == 2:
        index = index > 0
    return jnp.stack([lax.select_n(index, *[pieces[i ^ k] for k in count]) for i in count], 0)


def place_steps(pieces, index):
    out = jnp.zeros((len(pieces),) + pieces[0].shape, pieces[0].dtype)
    for step, piece in enumerate(pieces):
        out = lax.dynamic_update_index_in_dim(out, piece, index ^ step, 0)
    return out


def pieces_along(axis, value, count, up_only=False):
    pieces = [value]
    for step in range(1, count):
        routes = [(i, i ^ step) for i in range(count) if i < i ^ step or not up_only]
        pieces.append(lax.ppermute(value, axis, routes))
    return pieces


def gather_axis(value, axis, count):
    return place(pieces_along(axis, value, count), lax.axis_index(axis))


def total_of(parts):
    total = parts[0].astype(jnp.float32)
    for part in parts[1:]:
        total = total + part.astype(jnp.float32)
    return total


def add_up(parts):
    return total_of(parts).astype(jnp.bfloat16)


def parts_of(array, index, dim, count):
    return [pick(array, index ^ step, dim) for step in range(count)]


def send_parts(axis, parts, down_only=False):
    out = parts[:1]
    for step in range(1, len(parts)):
        routes = [(i, i ^ step) for i in range(len(parts)) if i ^ step < i or not down_only]
        out.append(lax.ppermute(parts[step], axis, routes))
    return out


def parts_along(axis, array, dim, count, down_only=False):
    return send_parts(axis, parts_of(array, lax.axis_index(axis), dim, count), down_only)


def hold(*values):
    return lax.optimization_barrier(values)


def tree_sum(value, axis, count):
    step = 1
    while step < count:
        value = value + swap(axis, value, count, step)
        step *= 2
    return value


def across(left, right, left_dim, right_dim):
    return lax.dot_general(
        left, right, (((left_dim,), (right_dim,)), ((), ())), preferred_element_type=jnp.float32
    )


def rotation(positions, rows):
    half = HD // 2
    freq = jnp.exp(jnp.arange(half, dtype=jnp.float32) * (-2.0 * math.log(BASE) / HD))
    angle = jnp.tile(freq[:, None] * positions.astype(jnp.float32)[None, :], (1, rows))
    return (jnp.cos(angle), jnp.sin(angle))


def turn(tensor, angles, sign):
    cosine, sine = angles[0], sign * angles[1]
    first, second = jnp.split(tensor.reshape(-1, 2, HD // 2, tensor.shape[-1]), 2, 1)
    return jnp.concatenate(
        [first * cosine - second * sine, second * cosine + first * sine], 1
    ).reshape(tensor.shape)


def attend_kernel(group, block, meta, q_ref, kv_ref, out_ref, log_ref, top, total, accum):
    ctx, length = meta[0], meta[1 + pl.program_id(1)]
    blocks_y = kv_ref.shape[0]
    top[...] = jnp.full(top.shape, NEG, jnp.float32)
    total[...] = jnp.zeros(total.shape, jnp.float32)
    accum[...] = jnp.zeros(accum.shape, jnp.float32)

    def step(index, masked):
        pair = kv_ref[index % blocks_y, index // blocks_y, 0, 0]
        keys = pair[:, :HD]
        values = pair.T[HD:]
        if masked:
            key_pos = index * block + lax.broadcasted_iota(jnp.int32, (block, block), 0)
            query_pos = ctx * block + lax.broadcasted_iota(jnp.int32, (block, block), 1)
            allowed = (key_pos <= query_pos) & (key_pos < length)
        heads = range(group)
        span = [slice(head * HD, (head + 1) * HD) for head in heads]
        scores = [
            jnp.dot(keys, q_ref[span[head]], preferred_element_type=jnp.float32) for head in heads
        ]
        if masked:
            scores = [jnp.where(allowed, part, NEG) for part in scores]
        old = top[...]
        new = jnp.maximum(
            old, jnp.concatenate([jnp.max(part, 0, keepdims=True) for part in scores], 0)
        )
        factor = jnp.exp(old - new)
        top[...] = new
        probs = [jnp.exp(scores[head] - new[head : head + 1]) for head in heads]
        total[...] = total[...] * factor + jnp.concatenate(
            [jnp.sum(part, 0, keepdims=True) for part in probs], 0
        )
        weighted = [
            jnp.dot(values, part.astype(jnp.bfloat16), preferred_element_type=jnp.float32)
            for part in probs
        ]
        for head in heads:
            accum[span[head]] = accum[span[head]] * factor[head : head + 1] + weighted[head]

    clear = jnp.minimum(ctx, length // block)
    last = jnp.minimum(ctx + 1, (length + block - 1) // block)
    pl.loop(0, clear)(lambda index: step(index, False))
    pl.loop(clear, last)(lambda index: step(index, True))
    for head in range(group):
        rows = slice(head * HD, (head + 1) * HD)
        out_ref[rows] = accum[rows] / total[head : head + 1]
    log_ref[0] = top[...] + jnp.log(total[...])


def attend_back_kernel(
    group, block, meta, q_ref, g_ref, out_ref, log_ref, kv_ref, dq_ref, dkv_ref, both, delta
):
    ctx, length = meta[0], meta[1 + pl.program_id(0)]
    blocks_y, blocks_z = kv_ref.shape[0], kv_ref.shape[1]
    dq_ref[...] = jnp.zeros(dq_ref.shape, jnp.float32)
    for head in range(group):
        rows = slice(head * HD, (head + 1) * HD)
        query, upper = q_ref[rows], g_ref[rows]
        both[head] = jnp.concatenate([query, upper], 0).T
        delta[head : head + 1] = jnp.sum(upper.astype(jnp.float32) * out_ref[rows], 0, keepdims=True)
    lane = lax.broadcasted_iota(jnp.int32, (block, 2 * HD), 1)

    def step(index, masked):
        pair = kv_ref[index % blocks_y, index // blocks_y, 0, 0]
        keys, values = pair[:, :HD], pair[:, HD:]
        keys_across = pair.T[:HD]
        if masked:
            key_pos = index * block + lax.broadcasted_iota(jnp.int32, (block, block), 0)
            query_pos = ctx * block + lax.broadcasted_iota(jnp.int32, (block, block), 1)
            allowed = (key_pos <= query_pos) & (key_pos < length)
        d_keys = jnp.zeros((block, 2 * HD), jnp.float32)
        d_values = jnp.zeros((block, 2 * HD), jnp.float32)
        heads = range(group)
        span = [slice(head * HD, (head + 1) * HD) for head in heads]
        scores = [
            jnp.dot(keys, q_ref[span[head]], preferred_element_type=jnp.float32) for head in heads
        ]
        d_probs = [
            jnp.dot(values, g_ref[span[head]], preferred_element_type=jnp.float32) for head in heads
        ]
        probs = [jnp.exp(scores[head] - log_ref[0, head : head + 1]) for head in heads]
        if masked:
            probs = [jnp.where(allowed, part, 0.0) for part in probs]
        d_scores = [
            (probs[head] * (d_probs[head] - delta[head : head + 1])).astype(jnp.bfloat16)
            for head in heads
        ]
        probs = [part.astype(jnp.bfloat16) for part in probs]
        d_query = [
            jnp.dot(keys_across, part, preferred_element_type=jnp.float32) for part in d_scores
        ]
        for head in heads:
            d_keys += jnp.dot(d_scores[head], both[head], preferred_element_type=jnp.float32)
        for head in heads:
            d_values += jnp.dot(probs[head], both[head], preferred_element_type=jnp.float32)
        for head in heads:
            dq_ref[span[head]] += d_query[head]
        merged = jnp.where(lane < HD, d_keys, d_values)
        dkv_ref[index % blocks_y, index // blocks_y, 0] = merged.astype(jnp.bfloat16)

    clear = jnp.minimum(ctx, length // block)
    last = jnp.minimum(ctx + 1, (length + block - 1) // block)
    pl.loop(0, clear)(lambda index: step(index, False))
    pl.loop(clear, last)(lambda index: step(index, True))

    @pl.loop(last, blocks_y * blocks_z)
    def _(index):
        dkv_ref[index % blocks_y, index // blocks_y, 0] = jnp.zeros(
            (block, 2 * HD), jnp.bfloat16
        )


def attention(meta, query, all_kv, block):
    ys, zs, _, rows, _, _ = all_kv.shape
    group = HEADS // KVH
    wide = pl.BlockSpec((group * HD, block), lambda h, r, meta: (h, r))
    pairs = pl.BlockSpec((ys, zs, 1, 1, block, 2 * HD), lambda h, r, meta: (0, 0, h, r, 0, 0))
    logs = pl.BlockSpec((1, group, block), lambda h, r, meta: (h, 0, r))
    return pl.pallas_call(
        functools.partial(attend_kernel, group, block),
        grid_spec=pltpu.PrefetchScalarGridSpec(
            num_scalar_prefetch=1,
            grid=(KVH, rows),
            in_specs=[wide, pairs],
            out_specs=[wide, logs],
            scratch_shapes=[
                pltpu.VMEM((group, block), jnp.float32),
                pltpu.VMEM((group, block), jnp.float32),
                pltpu.VMEM((group * HD, block), jnp.float32),
            ],
        ),
        out_shape=[
            jax.ShapeDtypeStruct((QD, rows * block), jnp.float32),
            jax.ShapeDtypeStruct((KVH, group, rows * block), jnp.float32),
        ],
        compiler_params=pltpu.CompilerParams(vmem_limit_bytes=32 * 2**20),
        cost_estimate=pl.CostEstimate(flops=1, bytes_accessed=1, transcendentals=0),
        name="attend",
    )(meta, query, all_kv)


def attention_back(h, meta, query, upper, attended, logs, all_kv, block):
    ys, zs, _, rows, _, _ = all_kv.shape
    group = HEADS // KVH
    wide = pl.BlockSpec((group * HD, block), lambda r, meta: (h, r))
    narrow = pl.BlockSpec((group * HD, block), lambda r, meta: (0, r))
    pairs = pl.BlockSpec((ys, zs, 1, 1, block, 2 * HD), lambda r, meta: (0, 0, h, r, 0, 0))
    terms = pl.BlockSpec((ys, zs, 1, block, 2 * HD), lambda r, meta: (0, 0, r, 0, 0))
    log_spec = pl.BlockSpec((1, group, block), lambda r, meta: (h, 0, r))
    return pl.pallas_call(
        functools.partial(attend_back_kernel, group, block),
        grid_spec=pltpu.PrefetchScalarGridSpec(
            num_scalar_prefetch=1,
            grid=(rows,),
            in_specs=[wide, wide, wide, log_spec, pairs],
            out_specs=[narrow, terms],
            scratch_shapes=[
                pltpu.VMEM((group, block, 2 * HD), jnp.bfloat16),
                pltpu.VMEM((group, block), jnp.float32),
            ],
        ),
        out_shape=[
            jax.ShapeDtypeStruct((group * HD, rows * block), jnp.float32),
            jax.ShapeDtypeStruct((ys, zs, rows, block, 2 * HD), jnp.bfloat16),
        ],
        compiler_params=pltpu.CompilerParams(vmem_limit_bytes=32 * 2**20),
        cost_estimate=pl.CostEstimate(flops=1, bytes_accessed=1, transcendentals=0),
        name="attend_back",
    )(meta, query, upper, attended, logs, all_kv)


def dot(left, right, left_dim=1, right_dim=0):
    return lax.dot_general(
        left, right, (((left_dim,), (right_dim,)), ((), ())), preferred_element_type=jnp.float32
    )


def hidden_kernel(xs, chunk, spot, n_own, n_other, u_own, u_other, first_a, first_b, *refs):
    seconds, (down_ref, inner_ref, d_ref, gate_ref, up_ref, across_ref) = refs[:xs], refs[xs:]
    y, x = spot[0], spot[1]
    count = n_own.shape[0]

    swapped = y != 0
    lower = [jnp.where(swapped, first_b[...], first_a[...]), jnp.where(swapped, first_a[...], first_b[...])]
    size = first_a.shape[1]
    for index, out in enumerate((gate_ref, up_ref)):
        for i in range(xs):
            out[2 * i * size : (2 * i + 1) * size] = lower[index][i]
            upper = seconds[i][index]
            for other in range(xs):
                if other != i:
                    upper = jnp.where((x ^ i) == other, seconds[other][index], upper)
            out[(2 * i + 1) * size : (2 * i + 2) * size] = upper

    @pl.when(pl.program_id(0) == 0)
    def _():
        for ref, columns in ((n_own, slice(0, count)), (n_other, slice(count, 2 * count))):
            turned = ref[...].T
            for i in range(xs):
                across_ref[i, :, columns] = turned[2 * i * size : (2 * i + 1) * size]
                across_ref[xs + (x ^ i), :, columns] = turned[(2 * i + 1) * size : (2 * i + 2) * size]

    gate_w, up_w, down_w = gate_ref[...], up_ref[...], down_ref[...]
    spans = [slice(i, i + chunk) for i in range(0, count, chunk)]
    gates = [dot(ref[span], gate_w) for ref in (n_own, n_other) for span in spans]
    ups = [dot(ref[span], up_w) for ref in (n_own, n_other) for span in spans]
    inners = [dot(ref[span], down_w, 1, 1) for ref in (u_own, u_other) for span in spans]
    parts = [slice(i, i + chunk) for i in range(0, 2 * count, chunk)]
    for part, gate, up, d_inner in zip(parts, gates, ups, inners):
        sigma = 1.0 / (1.0 + jnp.exp(-gate))
        activated = gate * sigma
        inner_ref[part] = (activated * up).astype(jnp.bfloat16)
        d_ref[1, part] = (d_inner * activated).astype(jnp.bfloat16)
        d_ref[0, part] = (d_inner * up * (sigma + activated * (1.0 - sigma))).astype(jnp.bfloat16)


def hidden_part(spot, normed, upper, first, second, down, width=256):
    count, size = normed[0].shape
    half = down.shape[0]
    xs, slab, _ = first[0].shape
    whole = pl.BlockSpec((count, size), lambda i, spot: (0, 0))
    lower = pl.BlockSpec((xs, slab, width), lambda i, spot: (0, 0, i))
    both = pl.BlockSpec((2, slab, width), lambda i, spot: (0, 0, i))
    columns = pl.BlockSpec((size, width), lambda i, spot: (0, i))
    rows = pl.BlockSpec((width, size), lambda i, spot: (i, 0))
    shapes = [(2 * count, half), (2, 2 * count, half), (size, half), (size, half)]
    shapes += [(2 * xs, slab, 2 * count)]
    return pl.pallas_call(
        functools.partial(hidden_kernel, xs, 256),
        grid_spec=pltpu.PrefetchScalarGridSpec(
            num_scalar_prefetch=1,
            grid=(pl.cdiv(half, width),),
            in_specs=[whole] * 4 + [lower] * 2 + [both] * xs + [rows],
            out_specs=[
                pl.BlockSpec((2 * count, width), lambda i, spot: (0, i)),
                pl.BlockSpec((2, 2 * count, width), lambda i, spot: (0, 0, i)),
                columns,
                columns,
                pl.BlockSpec((2 * xs, slab, 2 * count), lambda i, spot: (0, 0, 0)),
            ],
        ),
        out_shape=[jax.ShapeDtypeStruct(shape, jnp.bfloat16) for shape in shapes],
        compiler_params=pltpu.CompilerParams(vmem_limit_bytes=56 * 2**20),
        cost_estimate=pl.CostEstimate(flops=1, bytes_accessed=1, transcendentals=0),
        name="hidden",
    )(spot, *normed, *upper, *first, *second, down)


def grads_kernel(xs, spot, n_ref, d_own, d_other, *outs):
    y = spot[0]
    rows = n_ref.shape[1]
    features = n_ref[...].reshape(-1, n_ref.shape[2])
    for out, index, ref in zip(outs[:2], (y, 1 - y), (d_own, d_other)):
        result = dot(features, ref[...]).astype(jnp.bfloat16)
        out[...] = result[: xs * rows].reshape(out.shape)
        for step, upper in enumerate(outs[2:]):
            upper[index] = result[(xs + step) * rows : (xs + step + 1) * rows]


def gate_up_grads(spot, features, d_both, xs, start, stop, width):
    _, rows, count = features.shape
    first = start // width
    lower = pl.BlockSpec((xs, rows, width), lambda i, spot: (0, 0, i))
    upper = pl.BlockSpec((2, rows, width), lambda i, spot: (0, 0, i))
    return pl.pallas_call(
        functools.partial(grads_kernel, xs),
        grid_spec=pltpu.PrefetchScalarGridSpec(
            num_scalar_prefetch=1,
            grid=(pl.cdiv(stop - start, width),),
            in_specs=[
                pl.BlockSpec((2 * xs, rows, count), lambda i, spot: (0, 0, 0)),
                pl.BlockSpec((None, count, width), lambda i, spot: (spot[0], 0, first + i)),
                pl.BlockSpec((None, count, width), lambda i, spot: (1 - spot[0], 0, first + i)),
            ],
            out_specs=[lower] * 2 + [upper] * xs,
        ),
        out_shape=[jax.ShapeDtypeStruct((xs, rows, stop - start), jnp.bfloat16)] * 2
        + [jax.ShapeDtypeStruct((2, rows, stop - start), jnp.bfloat16)] * xs,
        compiler_params=pltpu.CompilerParams(vmem_limit_bytes=56 * 2**20),
        cost_estimate=pl.CostEstimate(flops=1, bytes_accessed=1, transcendentals=0),
        name="gate_up_grads",
    )(spot, features, d_both, d_both)


def down_kernel(inner_ref, u_own, u_other, out_ref):
    count = u_own.shape[0]
    result = dot(inner_ref[:count], u_own[...], 0, 0) + dot(inner_ref[count:], u_other[...], 0, 0)
    out_ref[...] = result.astype(jnp.bfloat16)


def down_grad(inner, upper, width=256):
    count, half = inner.shape
    size = upper[0].shape[1]
    return pl.pallas_call(
        down_kernel,
        grid=(pl.cdiv(half, width),),
        in_specs=[
            pl.BlockSpec((count, width), lambda i: (0, i)),
            pl.BlockSpec((count // 2, size), lambda i: (0, 0)),
            pl.BlockSpec((count // 2, size), lambda i: (0, 0)),
        ],
        out_specs=pl.BlockSpec((width, size), lambda i: (i, 0)),
        out_shape=jax.ShapeDtypeStruct((half, size), jnp.bfloat16),
        compiler_params=pltpu.CompilerParams(vmem_limit_bytes=56 * 2**20),
        cost_estimate=pl.CostEstimate(flops=1, bytes_accessed=1, transcendentals=0),
        name="down_grad",
    )(inner, *upper)


def back_kernel(half, d_ref, gate_ref, up_ref, own_ref, other_ref):
    step, width = pl.program_id(0), d_ref.shape[2]
    rest = half % width

    def add(limit, first):
        d_gate, d_up, gate, up = d_ref[0], d_ref[1], gate_ref[...], up_ref[...]
        if limit:
            d_gate, d_up, gate, up = (part[:, :limit] for part in (d_gate, d_up, gate, up))
        count = own_ref.shape[0]
        for out, rows in ((own_ref, slice(0, count)), (other_ref, slice(count, 2 * count))):
            result = dot(d_gate[rows], gate, 1, 1) + dot(d_up[rows], up, 1, 1)
            out[...] = result if first else out[...] + result

    last = pl.cdiv(half, width) - 1
    pl.when(step == 0)(lambda: add(0, True))
    pl.when((step > 0) & (step < last))(lambda: add(0, False))
    pl.when(step == last)(lambda: add(rest, False))


def hidden_back(d_both, gate, up, width=512):
    _, count, half = d_both.shape
    size = gate.shape[0]
    columns = pl.BlockSpec((size, width), lambda i: (0, i))
    whole = pl.BlockSpec((count // 2, size), lambda i: (0, 0))
    return pl.pallas_call(
        functools.partial(back_kernel, half),
        grid=(pl.cdiv(half, width),),
        in_specs=[pl.BlockSpec((2, count, width), lambda i: (0, 0, i)), columns, columns],
        out_specs=[whole, whole],
        out_shape=[jax.ShapeDtypeStruct((count // 2, size), jnp.float32)] * 2,
        compiler_params=pltpu.CompilerParams(vmem_limit_bytes=56 * 2**20),
        cost_estimate=pl.CostEstimate(flops=1, bytes_accessed=1, transcendentals=0),
        name="hidden_back",
    )(d_both, gate, up)


def project_kernel(inner_ref, down_ref, out_ref):
    out_ref[...] = dot(inner_ref[...], down_ref[...])


def project(inner, down, height=512):
    count, half = inner.shape
    size = down.shape[1]
    return pl.pallas_call(
        project_kernel,
        grid=(count // height,),
        in_specs=[
            pl.BlockSpec((height, half), lambda i: (i, 0)),
            pl.BlockSpec((half, size), lambda i: (0, 0)),
        ],
        out_specs=pl.BlockSpec((height, size), lambda i: (i, 0)),
        out_shape=jax.ShapeDtypeStruct((count, size), jnp.float32),
        compiler_params=pltpu.CompilerParams(vmem_limit_bytes=56 * 2**20),
        cost_estimate=pl.CostEstimate(flops=1, bytes_accessed=1, transcendentals=0),
        name="project",
    )(inner, down)


def layer(
    sizes,
    inputs,
    cotangent,
    lengths,
    qkv_weight,
    out_weight,
    gate_up_weight,
    down_weight,
    gains_biases,
    qkv_moment,
    qkv_square,
    out_moment,
    out_square,
    gate_up_moment,
    gate_up_square,
    down_moment,
    down_square,
    small_moment,
    small_square,
):
    xs, zs, ys = sizes
    everyone = ("x", "core", "z", "y")
    low = jnp.bfloat16
    rows, block_len, width = inputs.shape
    tokens = rows * block_len
    core, y_index = lax.axis_index("core"), lax.axis_index("y")
    ctx_index = lax.axis_index("z") * ys + y_index
    positions = ctx_index * block_len + jnp.arange(block_len, dtype=jnp.int32)
    kv_width = KVH * HD
    qkv_width = QD + 2 * kv_width
    scale = HD ** (-0.5)
    share = qkv_weight.shape[0]
    small_share = gains_biases.shape[0]
    ff_share = down_weight.shape[0]
    half = FF // 2
    x_index, z_index = lax.axis_index("x"), lax.axis_index("z")

    small_row = jnp.zeros((1, qkv_width), low).at[0, :small_share].set(gains_biases.astype(low))
    own_attn = jnp.concatenate([qkv_weight.astype(low), out_weight.astype(low)], 1)
    own_attn = jnp.concatenate([own_attn, jnp.pad(small_row, ((0, 0), (0, D)))], 0)
    other = swap("y", own_attn, ys, 1)
    lower = jnp.where(y_index == 0, own_attn, other)
    upper = jnp.where(y_index == 0, other, own_attn)
    pair_out = jnp.concatenate([lower[:share, qkv_width:], upper[:share, qkv_width:]], 0)
    lower, upper = lower[:, :qkv_width], upper[:, :qkv_width]
    spare = jnp.zeros((-2 * (share + 1) % 8, qkv_width), low)
    full_qkv = pieces_along(
        "z",
        jnp.concatenate([lower[:share], upper[:share], lower[share:], upper[share:], spare], 0),
        zs,
    )

    own_gu = (
        gate_up_weight.astype(low)
        .reshape(share, 2, xs, 2, zs, ys * ff_share)
        .transpose(3, 1, 0, 4, 2, 5)
        .reshape(4, share, half)
    )
    quad = core * 2 + y_index
    quads = place(
        [pick(own_gu, quad)]
        + [swap(("core", "y"), pick(own_gu, quad ^ step), 4, step) for step in range(1, 4)],
        quad,
    ).reshape(2, 2 * share, half)
    first = jnp.concatenate([quads[0], pair_out], 1)
    full_qkv, first, second = hold(full_qkv, first, quads[1])
    first = pieces_along("z", first, zs)
    full_qkv = pieces_along("x", place_steps(full_qkv, z_index), xs)
    full_qkv, first, second = hold(full_qkv, first, second)
    second = pieces_along("z", second, zs)
    first = pieces_along("x", place(first, z_index), xs)
    full_qkv = gather_axis(place(full_qkv, x_index), "core", 2).swapaxes(0, 1)
    full_small = full_qkv[..., 2 * share : 2 * share + ys, :small_share].reshape(-1)
    full_qkv = full_qkv[..., : 2 * share, :].reshape(D, qkv_width)

    small_used = full_small.astype(jnp.float32)
    gain_attn = small_used[:D]
    gain_mlp = small_used[D : 2 * D]
    bias = small_used[2 * D :]
    state = inputs.reshape(tokens, D).astype(jnp.float32)
    inverse_attn = lax.rsqrt(jnp.mean(state * state, -1, keepdims=True) + EPS)
    normed = (state * inverse_attn * gain_attn).astype(low)
    qkv = across(full_qkv, normed, 0, 1) + bias[:, None]
    angles = rotation(positions, rows)
    query = (turn(qkv[:QD], angles, 1.0) * scale).astype(low)
    keys = turn(qkv[QD : QD + kv_width], angles, 1.0).astype(low)
    values = qkv[QD + kv_width :].astype(low)
    own_kv = jnp.concatenate(
        [keys.reshape(KVH, HD, tokens), values.reshape(KVH, HD, tokens)], 1
    ).transpose(0, 2, 1)
    own_kv = own_kv.reshape(KVH, rows, block_len, 2 * HD)

    valid = (positions[None, :] < lengths[:, None]).astype(jnp.float32)
    upstream = cotangent.reshape(tokens, D).astype(jnp.float32) * valid.reshape(tokens, 1)

    own_kv, second, down_weight, upstream = hold(own_kv, second, down_weight, upstream)
    full_down = lax.all_gather(down_weight.astype(low), ("z", "x", "y"), axis=0, tiled=True)
    all_kv = pieces_along("z", own_kv, zs, True)
    second = pieces_along("y", place(second, z_index), ys)
    all_kv, first, second, upstream = hold(all_kv, first, second, upstream)
    all_kv = pieces_along("y", place(all_kv, z_index), ys)
    second = pieces_along("x", place(second, y_index), xs)
    first = place(first, x_index)
    first, full_out = first[..., :half], first[..., half:]
    all_kv, first, full_out, upstream = hold(all_kv, first, full_out, upstream)
    all_kv = place(all_kv, y_index)
    full_out = gather_axis(full_out, "core", 2).swapaxes(0, 1).reshape(QD, D)
    first = pieces_along("y", first, ys)
    meta = jnp.concatenate([ctx_index.astype(jnp.int32).reshape(1), lengths])
    attended, logs = attention(meta, query, all_kv, block_len)
    attended, first, second = hold(attended, first, second)
    spot = jnp.stack([y_index, x_index]).astype(jnp.int32)
    slab = D // (2 * xs)
    first = [part.reshape(xs, slab, half) for part in first]
    second = [part.reshape(2, slab, half) for part in second]
    mixed_low = attended.astype(low)
    hidden_state = state + across(mixed_low, full_out, 0, 0)
    inverse_mlp = lax.rsqrt(jnp.mean(hidden_state * hidden_state, -1, keepdims=True) + EPS)
    normed2 = (hidden_state * inverse_mlp * gain_mlp).astype(low)

    def pair(value):
        return value, swap("core", value, 2, 1)

    def pair_sum(value):
        return value[:tokens] + swap("core", value[tokens:], 2, 1)

    pair_up = pair(upstream.astype(low))
    pair_normed = pair(normed2)
    inner, d_both, full_gate, full_up, features = hidden_part(
        spot, pair_normed, pair_up, first, second, full_down
    )

    middle = half // 256 // 2 * 256 + 128

    def exchange(parts):
        first, second = list(parts[:2]), list(parts[2:])
        first[1] = swap("y", first[1], ys, 1)
        return first, second[:1] + [swap("x", second[i], xs, i) for i in range(1, xs)]

    left = gate_up_grads(spot, features, d_both, xs, 0, middle, 384)
    *left, d_both, inner = hold(*left, d_both, inner)
    left = exchange(left)
    right = gate_up_grads(spot, features, d_both, xs, middle, half, 384)
    grad_down = down_grad(inner, pair_up, 512)
    left, right, grad_down, d_both, inner = hold(left, right, grad_down, d_both, inner)
    red_down = lax.psum_scatter(grad_down, "z", scatter_dimension=0, tiled=True)
    output = project(inner, full_down)
    right = exchange(right)
    d_normed2 = hidden_back(d_both, full_gate, full_up)
    left, right, d_normed2, output = hold(left, right, d_normed2, output)
    first = jnp.concatenate([add_up(left[0]), add_up(right[0])], -1)
    second = jnp.concatenate([add_up(left[1]), add_up(right[1])], -1)
    d_normed2 = d_normed2[0] + swap("core", d_normed2[1], 2, 1)

    change_mlp, grad_gain_mlp = norm_back(hidden_state, inverse_mlp, gain_mlp, d_normed2)
    d_hidden = upstream + change_mlp
    d_hidden_low = d_hidden.astype(low)
    grad_out = across(mixed_low, d_hidden_low, 1, 0)
    d_mixed = across(full_out, d_hidden_low, 1, 1).astype(low)
    grad_out = parts_along(
        "core", grad_out.astype(low).reshape(xs, 2, zs, 2 * share, D), 1, 2
    )
    first, second = parts_of(first, x_index, 0, xs), parts_of(second, y_index, 0, ys)
    first, second, grad_out, d_mixed = hold(first, second, grad_out, d_mixed)
    first, second = send_parts("x", first), send_parts("y", second)
    d_query, kv_terms = [None] * KVH, [None] * KVH
    d_query[0], kv_terms[0] = attention_back(
        0, meta, query, d_mixed, attended, logs, all_kv, block_len
    )
    first, second, d_query[0], kv_terms[0], query = hold(
        first, second, d_query[0], kv_terms[0], query
    )
    red_quads = [add_up(part).reshape(zs, 2 * share, -1) for part in (first, second)]
    red_quads = parts_of(jnp.concatenate(red_quads, -1), z_index, 0, zs)
    grad_out = parts_of(add_up(grad_out), x_index, 0, xs)
    kv_terms[0] = parts_of(kv_terms[0], y_index, 0, ys)
    red_quads, grad_out, kv_terms[0], query = hold(red_quads, grad_out, kv_terms[0], query)
    red_quads, grad_out = send_parts("z", red_quads), send_parts("x", grad_out)
    kv_terms[0] = send_parts("y", kv_terms[0])
    d_query[1], kv_terms[1] = attention_back(
        1, meta, query, d_mixed, attended, logs, all_kv, block_len
    )
    red_quads, grad_out, kv_terms, d_query[1], red_down = hold(
        red_quads, grad_out, kv_terms, d_query[1], red_down
    )
    kv_terms[1] = parts_along("y", kv_terms[1], 0, ys)
    red_down = parts_along("x", red_down.reshape(xs, ys, ff_share, D), 0, xs)
    output = hidden_state + pair_sum(output)
    kv_terms, red_down, output, red_quads, grad_out = hold(
        kv_terms, red_down, output, red_quads, grad_out
    )
    kv_terms = jnp.stack([add_up(part) for part in kv_terms], 1)
    kv_terms = parts_along("z", kv_terms, 0, zs, True)
    kv_terms, red_quads, red_down, grad_out = hold(kv_terms, red_quads, red_down, grad_out)
    red_quads = add_up(red_quads)
    red_quads = jnp.stack([red_quads[:, :half], red_quads[:, half:]], 0)
    red_quads = parts_along("y", red_quads.reshape(2, ys, share, half), 1, ys)
    red_down = parts_along("y", add_up(red_down), 0, ys)
    red_out = parts_along("z", add_up(grad_out), 0, zs)
    kv_grads = total_of(kv_terms)
    red_gu = parts_along("core", place(red_quads, y_index), 1, 2)
    d_query = jnp.concatenate(d_query, 0)
    kv_grads = kv_grads.reshape(KVH, tokens, 2 * HD).transpose(0, 2, 1)
    d_qkv = jnp.concatenate(
        [
            turn(d_query * scale, angles, -1.0),
            turn(kv_grads[:, :HD].reshape(kv_width, tokens), angles, -1.0),
            kv_grads[:, HD:].reshape(kv_width, tokens),
        ],
        0,
    ).astype(low)
    grad_bias = jnp.sum(d_qkv.astype(jnp.float32), 1)
    grad_qkv = across(normed, d_qkv, 0, 1)
    d_normed = across(d_qkv, full_qkv, 0, 1)
    change_attn, grad_gain_attn = norm_back(state, inverse_attn, gain_attn, d_normed)
    input_grad = (d_hidden + change_attn).astype(low)
    grad_small = jnp.concatenate([grad_gain_attn, grad_gain_mlp, grad_bias])

    grad_small = grad_small.astype(low).reshape(-1, ys, small_share)
    grad_small = jnp.pad(grad_small, ((0, 0), (0, 8 - ys), (0, qkv_width - small_share)))
    grad_qkv = jnp.concatenate(
        [grad_qkv.astype(low).reshape(-1, ys * share, qkv_width), grad_small], 1
    )
    red_qkv = grad_qkv.reshape(xs, 2, zs, -1, qkv_width)
    red_qkv = add_up(parts_along("core", red_qkv, 1, 2))
    red_qkv = parts_along("x", red_qkv, 0, xs)
    red_qkv, red_gu, red_out, red_down = hold(red_qkv, red_gu, red_out, red_down)
    red_out = add_up(red_out)
    red_qkv = add_up(parts_along("z", add_up(red_qkv), 0, zs))
    red_down = total_of(red_down)

    red_small = red_qkv[ys * share : ys * share + ys]
    red_qkv = red_qkv[: ys * share].reshape(ys, share, qkv_width)
    red_out = red_out.reshape(ys, share, D)
    along = jnp.zeros((ys, -share % 8, qkv_width + D), low)
    along = along.at[:, 0, :qkv_width].set(red_small)
    along = jnp.concatenate([jnp.concatenate([red_qkv, red_out], 2), along], 1)
    mine = pick(along, y_index).astype(jnp.float32)
    mine = mine + swap("y", pick(along, 1 - y_index), ys, 1).astype(jnp.float32)
    red_qkv, red_out = mine[:share, :qkv_width], mine[:share, qkv_width:]
    red_small = mine[share, :small_share]
    red_gu = place(red_gu, core)
    red_gu = (
        red_gu.reshape(2, 2, share, zs, xs, ys * ff_share)
        .transpose(2, 1, 4, 0, 3, 5)
        .reshape(share, 2 * FF)
        .astype(jnp.float32)
    )

    red_gu, red_qkv, red_out, red_small = hold(red_gu, red_qkv, red_out, red_small)
    local_square = (
        jnp.sum(red_qkv * red_qkv)
        + jnp.sum(red_out * red_out)
        + jnp.sum(red_gu * red_gu)
        + jnp.sum(red_down * red_down)
        + jnp.sum(red_small * red_small)
    ).reshape(1)
    square_sum = local_square
    for axis, count in (("core", 2), ("y", ys), ("x", xs), ("z", zs)):
        square_sum = tree_sum(square_sum, axis, count)
    square_sum = square_sum[0]
    grad_norm = jnp.sqrt(square_sum)
    factor = CLIP / jnp.maximum(grad_norm, CLIP)
    qkv_new = adam_step(red_qkv, qkv_moment, qkv_square, qkv_weight, factor, RATES[0], DECAYS[0])
    out_new = adam_step(red_out, out_moment, out_square, out_weight, factor, RATES[1], DECAYS[1])
    gu_new = adam_step(
        red_gu, gate_up_moment, gate_up_square, gate_up_weight, factor, RATES[2], DECAYS[2]
    )
    down_new = adam_step(
        red_down, down_moment, down_square, down_weight, factor, RATES[3], DECAYS[3]
    )
    small_new = adam_step(
        red_small, small_moment, small_square, gains_biases, factor, RATES[4], DECAYS[4]
    )
    return (
        output.astype(low).reshape(inputs.shape),
        input_grad.reshape(inputs.shape),
        grad_norm,
        *qkv_new,
        *out_new,
        *gu_new,
        *down_new,
        *small_new,
    )


def solution(mesh):
    dp, ctx = mesh.shape["dp"], mesh.shape["ctx"]
    sizes = (dp // 2, ctx // 2, 2)
    fine = Mesh(mesh.devices.reshape(dp // 2, 2, ctx // 2, 2), ("x", "core", "z", "y"))
    seqs, blocks = ("x", "core"), ("z", "y")
    token = P(seqs, blocks, None)
    matrix = P(seqs + blocks, None)
    vector = P(seqs + blocks)
    weights = (matrix,) * 4 + (vector,)
    states = (matrix,) * 8 + (vector,) * 2
    return jax.shard_map(
        functools.partial(layer, sizes),
        mesh=fine,
        in_specs=(token, token, P(seqs)) + weights + states,
        out_specs=(token, token, P()) + (matrix,) * 16 + (vector,) * 4,
        check_vma=False,
    )
```

```python
import functools
import math

import jax
import jax.numpy as jnp
from jax import lax
from jax.experimental import pallas as pl
from jax.experimental.pallas import tpu as pltpu
from jax.sharding import Mesh
from jax.sharding import PartitionSpec as P

D = 896
HEADS = 14
KVH = 2
HD = 64
FF = 4864
STEP = 5
QD = 896


EPS = 1e-06
NEG = -1e30
BASE = 1000000.0
CLIP = 1.0
BETA_ONE = 0.9
BETA_TWO = 0.95
ADAM_EPS = 1e-08
RATES = (0.06, 1.0, 0.06, 0.03, 3.0)
DECAYS = (0.1, 0.1, 0.1, 0.1, 0.0)


def norm_back(state, inverse, gain, upstream):
    scaled = gain * upstream
    change = inverse * scaled - state * inverse**3 * jnp.mean(scaled * state, -1, keepdims=True)
    gain_grad = jnp.sum((upstream * state * inverse).reshape(-1, state.shape[-1]), 0)
    return (change, gain_grad)


def adam_step(gradient, moment, square, weight, factor, rate, decay):
    gradient = gradient * factor
    moment = BETA_ONE * moment + (1.0 - BETA_ONE) * gradient
    square = BETA_TWO * square + (1.0 - BETA_TWO) * gradient * gradient
    corr_one = 1.0 - BETA_ONE**STEP
    corr_two = 1.0 - BETA_TWO**STEP
    update = moment / corr_one / (jnp.sqrt(square / corr_two) + ADAM_EPS)
    weight = weight * (1.0 - rate * decay) - rate * update
    return (gradient, moment, square, weight)


def swap(axis, value, count, step):
    return lax.ppermute(value, axis, [(i, i ^ step) for i in range(count)])


def pick(array, index, dim=0):
    return lax.dynamic_index_in_dim(array, index, dim, keepdims=False)


def place(pieces, index):
    count = range(len(pieces))
    index = index.astype(jnp.int32)
    if len(pieces) == 2:
        index = index > 0
    return jnp.stack([lax.select_n(index, *[pieces[i ^ k] for k in count]) for i in count], 0)


def place_steps(pieces, index):
    out = jnp.zeros((len(pieces),) + pieces[0].shape, pieces[0].dtype)
    for step, piece in enumerate(pieces):
        out = lax.dynamic_update_index_in_dim(out, piece, index ^ step, 0)
    return out


def pieces_along(axis, value, count, up_only=False):
    pieces = [value]
    for step in range(1, count):
        routes = [(i, i ^ step) for i in range(count) if i < i ^ step or not up_only]
        pieces.append(lax.ppermute(value, axis, routes))
    return pieces


def gather_axis(value, axis, count):
    return place(pieces_along(axis, value, count), lax.axis_index(axis))


def total_of(parts):
    total = parts[0].astype(jnp.float32)
    for part in parts[1:]:
        total = total + part.astype(jnp.float32)
    return total


def add_up(parts):
    return total_of(parts).astype(jnp.bfloat16)


def parts_of(array, index, dim, count):
    return [pick(array, index ^ step, dim) for step in range(count)]


def sums_of(groups, index, count):
    return [
        jnp.concatenate([add_up([pick(part, index ^ step) for part in group]) for group in groups], -1)
        for step in range(count)
    ]


def send_parts(axis, parts, down_only=False):
    out = parts[:1]
    for step in range(1, len(parts)):
        routes = [(i, i ^ step) for i in range(len(parts)) if i ^ step < i or not down_only]
        out.append(lax.ppermute(parts[step], axis, routes))
    return out


def parts_along(axis, array, dim, count, down_only=False):
    return send_parts(axis, parts_of(array, lax.axis_index(axis), dim, count), down_only)


def hold(*values):
    return lax.optimization_barrier(values)


def tree_sum(value, axis, count):
    step = 1
    while step < count:
        value = value + swap(axis, value, count, step)
        step *= 2
    return value


def across(left, right, left_dim, right_dim):
    return lax.dot_general(
        left, right, (((left_dim,), (right_dim,)), ((), ())), preferred_element_type=jnp.float32
    )


def rotation(positions, rows):
    half = HD // 2
    freq = jnp.exp(jnp.arange(half, dtype=jnp.float32) * (-2.0 * math.log(BASE) / HD))
    angle = jnp.tile(freq[:, None] * positions.astype(jnp.float32)[None, :], (1, rows))
    return (jnp.cos(angle), jnp.sin(angle))


def turn(tensor, angles, sign):
    cosine, sine = angles[0], sign * angles[1]
    first, second = jnp.split(tensor.reshape(-1, 2, HD // 2, tensor.shape[-1]), 2, 1)
    return jnp.concatenate(
        [first * cosine - second * sine, second * cosine + first * sine], 1
    ).reshape(tensor.shape)


def attend_kernel(group, block, meta, q_ref, kv_ref, out_ref, log_ref, top, total, accum):
    ctx, length = meta[0], meta[1 + pl.program_id(1)]
    blocks_y = kv_ref.shape[0]
    top[...] = jnp.full(top.shape, NEG, jnp.float32)
    total[...] = jnp.zeros(total.shape, jnp.float32)
    accum[...] = jnp.zeros(accum.shape, jnp.float32)

    def step(index, masked):
        pair = kv_ref[index % blocks_y, index // blocks_y, 0, 0]
        keys = pair[:, :HD]
        values = pair.T[HD:]
        if masked:
            key_pos = index * block + lax.broadcasted_iota(jnp.int32, (block, block), 0)
            query_pos = ctx * block + lax.broadcasted_iota(jnp.int32, (block, block), 1)
            allowed = (key_pos <= query_pos) & (key_pos < length)
        heads = range(group)
        span = [slice(head * HD, (head + 1) * HD) for head in heads]
        scores = [
            jnp.dot(keys, q_ref[span[head]], preferred_element_type=jnp.float32) for head in heads
        ]
        if masked:
            scores = [jnp.where(allowed, part, NEG) for part in scores]
        old = top[...]
        new = jnp.maximum(
            old, jnp.concatenate([jnp.max(part, 0, keepdims=True) for part in scores], 0)
        )
        factor = jnp.exp(old - new)
        top[...] = new
        probs = [jnp.exp(scores[head] - new[head : head + 1]) for head in heads]
        total[...] = total[...] * factor + jnp.concatenate(
            [jnp.sum(part, 0, keepdims=True) for part in probs], 0
        )
        weighted = [
            jnp.dot(values, part.astype(jnp.bfloat16), preferred_element_type=jnp.float32)
            for part in probs
        ]
        for head in heads:
            accum[span[head]] = accum[span[head]] * factor[head : head + 1] + weighted[head]

    clear = jnp.minimum(ctx, length // block)
    last = jnp.minimum(ctx + 1, (length + block - 1) // block)
    pl.loop(0, clear)(lambda index: step(index, False))
    pl.loop(clear, last)(lambda index: step(index, True))
    for head in range(group):
        rows = slice(head * HD, (head + 1) * HD)
        out_ref[rows] = accum[rows] / total[head : head + 1]
    log_ref[0] = top[...] + jnp.log(total[...])


def attend_back_kernel(
    group, block, meta, q_ref, g_ref, out_ref, log_ref, kv_ref, dq_ref, dkv_ref, both, delta
):
    ctx, length = meta[0], meta[1 + pl.program_id(0)]
    blocks_y, blocks_z = kv_ref.shape[0], kv_ref.shape[1]
    dq_ref[...] = jnp.zeros(dq_ref.shape, jnp.float32)
    for head in range(group):
        rows = slice(head * HD, (head + 1) * HD)
        query, upper = q_ref[rows], g_ref[rows]
        both[head] = jnp.concatenate([query, upper], 0).T
        delta[head : head + 1] = jnp.sum(upper.astype(jnp.float32) * out_ref[rows], 0, keepdims=True)
    lane = lax.broadcasted_iota(jnp.int32, (block, 2 * HD), 1)

    def step(index, masked):
        pair = kv_ref[index % blocks_y, index // blocks_y, 0, 0]
        keys, values = pair[:, :HD], pair[:, HD:]
        keys_across = pair.T[:HD]
        if masked:
            key_pos = index * block + lax.broadcasted_iota(jnp.int32, (block, block), 0)
            query_pos = ctx * block + lax.broadcasted_iota(jnp.int32, (block, block), 1)
            allowed = (key_pos <= query_pos) & (key_pos < length)
        d_keys = jnp.zeros((block, 2 * HD), jnp.float32)
        d_values = jnp.zeros((block, 2 * HD), jnp.float32)
        heads = range(group)
        span = [slice(head * HD, (head + 1) * HD) for head in heads]
        scores = [
            jnp.dot(keys, q_ref[span[head]], preferred_element_type=jnp.float32) for head in heads
        ]
        d_probs = [
            jnp.dot(values, g_ref[span[head]], preferred_element_type=jnp.float32) for head in heads
        ]
        probs = [jnp.exp(scores[head] - log_ref[0, head : head + 1]) for head in heads]
        if masked:
            probs = [jnp.where(allowed, part, 0.0) for part in probs]
        d_scores = [
            (probs[head] * (d_probs[head] - delta[head : head + 1])).astype(jnp.bfloat16)
            for head in heads
        ]
        probs = [part.astype(jnp.bfloat16) for part in probs]
        d_query = [
            jnp.dot(keys_across, part, preferred_element_type=jnp.float32) for part in d_scores
        ]
        for head in heads:
            d_keys += jnp.dot(d_scores[head], both[head], preferred_element_type=jnp.float32)
        for head in heads:
            d_values += jnp.dot(probs[head], both[head], preferred_element_type=jnp.float32)
        for head in heads:
            dq_ref[span[head]] += d_query[head]
        merged = jnp.where(lane < HD, d_keys, d_values)
        dkv_ref[index % blocks_y, index // blocks_y, 0] = merged.astype(jnp.bfloat16)

    clear = jnp.minimum(ctx, length // block)
    last = jnp.minimum(ctx + 1, (length + block - 1) // block)
    pl.loop(0, clear)(lambda index: step(index, False))
    pl.loop(clear, last)(lambda index: step(index, True))

    @pl.loop(last, blocks_y * blocks_z)
    def _(index):
        dkv_ref[index % blocks_y, index // blocks_y, 0] = jnp.zeros(
            (block, 2 * HD), jnp.bfloat16
        )


def attention(meta, query, all_kv, block):
    ys, zs, _, rows, _, _ = all_kv.shape
    group = HEADS // KVH
    wide = pl.BlockSpec((group * HD, block), lambda h, r, meta: (h, r))
    pairs = pl.BlockSpec((ys, zs, 1, 1, block, 2 * HD), lambda h, r, meta: (0, 0, h, r, 0, 0))
    logs = pl.BlockSpec((1, group, block), lambda h, r, meta: (h, 0, r))
    return pl.pallas_call(
        functools.partial(attend_kernel, group, block),
        grid_spec=pltpu.PrefetchScalarGridSpec(
            num_scalar_prefetch=1,
            grid=(KVH, rows),
            in_specs=[wide, pairs],
            out_specs=[wide, logs],
            scratch_shapes=[
                pltpu.VMEM((group, block), jnp.float32),
                pltpu.VMEM((group, block), jnp.float32),
                pltpu.VMEM((group * HD, block), jnp.float32),
            ],
        ),
        out_shape=[
            jax.ShapeDtypeStruct((QD, rows * block), jnp.float32),
            jax.ShapeDtypeStruct((KVH, group, rows * block), jnp.float32),
        ],
        compiler_params=pltpu.CompilerParams(vmem_limit_bytes=32 * 2**20),
        cost_estimate=pl.CostEstimate(flops=1, bytes_accessed=1, transcendentals=0),
        name="attend",
    )(meta, query, all_kv)


def attention_back(h, meta, query, upper, attended, logs, all_kv, block):
    ys, zs, _, rows, _, _ = all_kv.shape
    group = HEADS // KVH
    wide = pl.BlockSpec((group * HD, block), lambda r, meta: (h, r))
    narrow = pl.BlockSpec((group * HD, block), lambda r, meta: (0, r))
    pairs = pl.BlockSpec((ys, zs, 1, 1, block, 2 * HD), lambda r, meta: (0, 0, h, r, 0, 0))
    terms = pl.BlockSpec((ys, zs, 1, block, 2 * HD), lambda r, meta: (0, 0, r, 0, 0))
    log_spec = pl.BlockSpec((1, group, block), lambda r, meta: (h, 0, r))
    return pl.pallas_call(
        functools.partial(attend_back_kernel, group, block),
        grid_spec=pltpu.PrefetchScalarGridSpec(
            num_scalar_prefetch=1,
            grid=(rows,),
            in_specs=[wide, wide, wide, log_spec, pairs],
            out_specs=[narrow, terms],
            scratch_shapes=[
                pltpu.VMEM((group, block, 2 * HD), jnp.bfloat16),
                pltpu.VMEM((group, block), jnp.float32),
            ],
        ),
        out_shape=[
            jax.ShapeDtypeStruct((group * HD, rows * block), jnp.float32),
            jax.ShapeDtypeStruct((ys, zs, rows, block, 2 * HD), jnp.bfloat16),
        ],
        compiler_params=pltpu.CompilerParams(vmem_limit_bytes=32 * 2**20),
        cost_estimate=pl.CostEstimate(flops=1, bytes_accessed=1, transcendentals=0),
        name="attend_back",
    )(meta, query, upper, attended, logs, all_kv)


def dot(left, right, left_dim=1, right_dim=0):
    return lax.dot_general(
        left, right, (((left_dim,), (right_dim,)), ((), ())), preferred_element_type=jnp.float32
    )


def hidden_kernel(xs, chunk, spot, n_own, n_other, u_own, u_other, first_a, first_b, *refs):
    seconds, (down_ref, inner_ref, d_ref, gate_ref, up_ref, across_ref) = refs[:xs], refs[xs:]
    y, x = spot[0], spot[1]
    count = n_own.shape[0]

    swapped = y != 0
    lower = [jnp.where(swapped, first_b[...], first_a[...]), jnp.where(swapped, first_a[...], first_b[...])]
    size = first_a.shape[1]
    for index, out in enumerate((gate_ref, up_ref)):
        for i in range(xs):
            out[2 * i * size : (2 * i + 1) * size] = lower[index][i]
            upper = seconds[i][index]
            for other in range(xs):
                if other != i:
                    upper = jnp.where((x ^ i) == other, seconds[other][index], upper)
            out[(2 * i + 1) * size : (2 * i + 2) * size] = upper

    @pl.when(pl.program_id(0) == 0)
    def _():
        for ref, columns in ((n_own, slice(0, count)), (n_other, slice(count, 2 * count))):
            turned = ref[...].T
            for i in range(xs):
                across_ref[i, :, columns] = turned[2 * i * size : (2 * i + 1) * size]
                across_ref[xs + (x ^ i), :, columns] = turned[(2 * i + 1) * size : (2 * i + 2) * size]

    gate_w, up_w, down_w = gate_ref[...], up_ref[...], down_ref[...]
    spans = [slice(i, i + chunk) for i in range(0, count, chunk)]
    gates = [dot(ref[span], gate_w) for ref in (n_own, n_other) for span in spans]
    ups = [dot(ref[span], up_w) for ref in (n_own, n_other) for span in spans]
    inners = [dot(ref[span], down_w, 1, 1) for ref in (u_own, u_other) for span in spans]
    parts = [slice(i, i + chunk) for i in range(0, 2 * count, chunk)]
    for part, gate, up, d_inner in zip(parts, gates, ups, inners):
        sigma = 1.0 / (1.0 + jnp.exp(-gate))
        activated = gate * sigma
        inner_ref[part] = (activated * up).astype(jnp.bfloat16)
        d_ref[1, part] = (d_inner * activated).astype(jnp.bfloat16)
        d_ref[0, part] = (d_inner * up * (sigma + activated * (1.0 - sigma))).astype(jnp.bfloat16)


def hidden_part(spot, normed, upper, first, second, down, width=256):
    count, size = normed[0].shape
    half = down.shape[0]
    xs, slab, _ = first[0].shape
    whole = pl.BlockSpec((count, size), lambda i, spot: (0, 0))
    lower = pl.BlockSpec((xs, slab, width), lambda i, spot: (0, 0, i))
    both = pl.BlockSpec((2, slab, width), lambda i, spot: (0, 0, i))
    columns = pl.BlockSpec((size, width), lambda i, spot: (0, i))
    rows = pl.BlockSpec((width, size), lambda i, spot: (i, 0))
    shapes = [(2 * count, half), (2, 2 * count, half), (size, half), (size, half)]
    shapes += [(2 * xs, slab, 2 * count)]
    return pl.pallas_call(
        functools.partial(hidden_kernel, xs, 256),
        grid_spec=pltpu.PrefetchScalarGridSpec(
            num_scalar_prefetch=1,
            grid=(pl.cdiv(half, width),),
            in_specs=[whole] * 4 + [lower] * 2 + [both] * xs + [rows],
            out_specs=[
                pl.BlockSpec((2 * count, width), lambda i, spot: (0, i)),
                pl.BlockSpec((2, 2 * count, width), lambda i, spot: (0, 0, i)),
                columns,
                columns,
                pl.BlockSpec((2 * xs, slab, 2 * count), lambda i, spot: (0, 0, 0)),
            ],
        ),
        out_shape=[jax.ShapeDtypeStruct(shape, jnp.bfloat16) for shape in shapes],
        compiler_params=pltpu.CompilerParams(vmem_limit_bytes=56 * 2**20),
        cost_estimate=pl.CostEstimate(flops=1, bytes_accessed=1, transcendentals=0),
        name="hidden",
    )(spot, *normed, *upper, *first, *second, down)


def grads_kernel(xs, spot, n_ref, d_own, d_other, *outs):
    y = spot[0]
    rows = n_ref.shape[1]
    features = n_ref[...].reshape(-1, n_ref.shape[2])
    for out, index, ref in zip(outs[:2], (y, 1 - y), (d_own, d_other)):
        result = dot(features, ref[...]).astype(jnp.bfloat16)
        out[...] = result[: xs * rows].reshape(out.shape)
        for step, upper in enumerate(outs[2:]):
            upper[index] = result[(xs + step) * rows : (xs + step + 1) * rows]


def gate_up_grads(spot, features, d_both, xs, start, stop, width):
    _, rows, count = features.shape
    first = start // width
    lower = pl.BlockSpec((xs, rows, width), lambda i, spot: (0, 0, i))
    upper = pl.BlockSpec((2, rows, width), lambda i, spot: (0, 0, i))
    return pl.pallas_call(
        functools.partial(grads_kernel, xs),
        grid_spec=pltpu.PrefetchScalarGridSpec(
            num_scalar_prefetch=1,
            grid=(pl.cdiv(stop - start, width),),
            in_specs=[
                pl.BlockSpec((2 * xs, rows, count), lambda i, spot: (0, 0, 0)),
                pl.BlockSpec((None, count, width), lambda i, spot: (spot[0], 0, first + i)),
                pl.BlockSpec((None, count, width), lambda i, spot: (1 - spot[0], 0, first + i)),
            ],
            out_specs=[lower] * 2 + [upper] * xs,
        ),
        out_shape=[jax.ShapeDtypeStruct((xs, rows, stop - start), jnp.bfloat16)] * 2
        + [jax.ShapeDtypeStruct((2, rows, stop - start), jnp.bfloat16)] * xs,
        compiler_params=pltpu.CompilerParams(vmem_limit_bytes=56 * 2**20),
        cost_estimate=pl.CostEstimate(flops=1, bytes_accessed=1, transcendentals=0),
        name="gate_up_grads",
    )(spot, features, d_both, d_both)


def down_kernel(inner_ref, u_own, u_other, out_ref):
    count = u_own.shape[0]
    result = dot(inner_ref[:count], u_own[...], 0, 0) + dot(inner_ref[count:], u_other[...], 0, 0)
    out_ref[...] = result.astype(jnp.bfloat16)


def down_grad(inner, upper, width=256):
    count, half = inner.shape
    size = upper[0].shape[1]
    return pl.pallas_call(
        down_kernel,
        grid=(pl.cdiv(half, width),),
        in_specs=[
            pl.BlockSpec((count, width), lambda i: (0, i)),
            pl.BlockSpec((count // 2, size), lambda i: (0, 0)),
            pl.BlockSpec((count // 2, size), lambda i: (0, 0)),
        ],
        out_specs=pl.BlockSpec((width, size), lambda i: (i, 0)),
        out_shape=jax.ShapeDtypeStruct((half, size), jnp.bfloat16),
        compiler_params=pltpu.CompilerParams(vmem_limit_bytes=56 * 2**20),
        cost_estimate=pl.CostEstimate(flops=1, bytes_accessed=1, transcendentals=0),
        name="down_grad",
    )(inner, *upper)


def back_kernel(half, d_ref, gate_ref, up_ref, own_ref, other_ref):
    step, width = pl.program_id(0), d_ref.shape[2]
    rest = half % width

    def add(limit, first):
        d_gate, d_up, gate, up = d_ref[0], d_ref[1], gate_ref[...], up_ref[...]
        if limit:
            d_gate, d_up, gate, up = (part[:, :limit] for part in (d_gate, d_up, gate, up))
        count = own_ref.shape[0]
        for out, rows in ((own_ref, slice(0, count)), (other_ref, slice(count, 2 * count))):
            result = dot(d_gate[rows], gate, 1, 1) + dot(d_up[rows], up, 1, 1)
            out[...] = result if first else out[...] + result

    last = pl.cdiv(half, width) - 1
    pl.when(step == 0)(lambda: add(0, True))
    pl.when((step > 0) & (step < last))(lambda: add(0, False))
    pl.when(step == last)(lambda: add(rest, False))


def hidden_back(d_both, gate, up, width=512):
    _, count, half = d_both.shape
    size = gate.shape[0]
    columns = pl.BlockSpec((size, width), lambda i: (0, i))
    whole = pl.BlockSpec((count // 2, size), lambda i: (0, 0))
    return pl.pallas_call(
        functools.partial(back_kernel, half),
        grid=(pl.cdiv(half, width),),
        in_specs=[pl.BlockSpec((2, count, width), lambda i: (0, 0, i)), columns, columns],
        out_specs=[whole, whole],
        out_shape=[jax.ShapeDtypeStruct((count // 2, size), jnp.float32)] * 2,
        compiler_params=pltpu.CompilerParams(vmem_limit_bytes=56 * 2**20),
        cost_estimate=pl.CostEstimate(flops=1, bytes_accessed=1, transcendentals=0),
        name="hidden_back",
    )(d_both, gate, up)


def project_kernel(inner_ref, down_ref, out_ref):
    out_ref[...] = dot(inner_ref[...], down_ref[...])


def project(inner, down, height=512):
    count, half = inner.shape
    size = down.shape[1]
    return pl.pallas_call(
        project_kernel,
        grid=(count // height,),
        in_specs=[
            pl.BlockSpec((height, half), lambda i: (i, 0)),
            pl.BlockSpec((half, size), lambda i: (0, 0)),
        ],
        out_specs=pl.BlockSpec((height, size), lambda i: (i, 0)),
        out_shape=jax.ShapeDtypeStruct((count, size), jnp.float32),
        compiler_params=pltpu.CompilerParams(vmem_limit_bytes=56 * 2**20),
        cost_estimate=pl.CostEstimate(flops=1, bytes_accessed=1, transcendentals=0),
        name="project",
    )(inner, down)


def norm_kernel(
    own_ref, other_ref, state_ref, upstream_ref, inverse_ref, gain_ref, weight_ref, mixed_ref,
    hidden_ref, gain_grad_ref, mixed_grad_ref, weight_grad_ref,
):
    incoming, state, inverse = own_ref[...] + other_ref[...], state_ref[...], inverse_ref[...]
    scaled = gain_ref[...] * incoming
    mean = jnp.mean(scaled * state, -1, keepdims=True)
    hidden = upstream_ref[...] + (inverse * scaled - state * inverse**3 * mean)
    gain_grad_ref[...] = jnp.sum(incoming * state * inverse, 0, keepdims=True)
    hidden_ref[...] = hidden
    low = hidden.astype(jnp.bfloat16)
    mixed_grad_ref[...] = dot(weight_ref[...], low, 1, 1).astype(jnp.bfloat16)
    weight_grad_ref[...] = dot(mixed_ref[...], low).astype(jnp.bfloat16)


def norm_and_out_back(own, other, state, upstream, inverse, gain, weight, mixed):
    count, size = state.shape
    return pl.pallas_call(
        norm_kernel,
        out_shape=[
            jax.ShapeDtypeStruct((count, size), jnp.float32),
            jax.ShapeDtypeStruct((1, size), jnp.float32),
            jax.ShapeDtypeStruct((weight.shape[0], count), jnp.bfloat16),
            jax.ShapeDtypeStruct(weight.shape, jnp.bfloat16),
        ],
        compiler_params=pltpu.CompilerParams(vmem_limit_bytes=48 * 2**20),
        cost_estimate=pl.CostEstimate(flops=1, bytes_accessed=1, transcendentals=0),
        name="norm_and_out_back",
    )(own, other, state, upstream, inverse, gain[None, :], weight, mixed)


def layer(
    sizes,
    inputs,
    cotangent,
    lengths,
    qkv_weight,
    out_weight,
    gate_up_weight,
    down_weight,
    gains_biases,
    qkv_moment,
    qkv_square,
    out_moment,
    out_square,
    gate_up_moment,
    gate_up_square,
    down_moment,
    down_square,
    small_moment,
    small_square,
):
    xs, zs, ys = sizes
    everyone = ("x", "core", "z", "y")
    low = jnp.bfloat16
    rows, block_len, width = inputs.shape
    tokens = rows * block_len
    core, y_index = lax.axis_index("core"), lax.axis_index("y")
    ctx_index = lax.axis_index("z") * ys + y_index
    positions = ctx_index * block_len + jnp.arange(block_len, dtype=jnp.int32)
    kv_width = KVH * HD
    qkv_width = QD + 2 * kv_width
    scale = HD ** (-0.5)
    share = qkv_weight.shape[0]
    small_share = gains_biases.shape[0]
    ff_share = down_weight.shape[0]
    half = FF // 2
    x_index, z_index = lax.axis_index("x"), lax.axis_index("z")

    small_row = jnp.zeros((1, qkv_width), low).at[0, :small_share].set(gains_biases.astype(low))
    own_attn = jnp.concatenate([qkv_weight.astype(low), out_weight.astype(low)], 1)
    own_attn = jnp.concatenate([own_attn, jnp.pad(small_row, ((0, 0), (0, D)))], 0)
    other = swap("y", own_attn, ys, 1)
    lower = jnp.where(y_index == 0, own_attn, other)
    upper = jnp.where(y_index == 0, other, own_attn)
    pair_out = jnp.concatenate([lower[:share, qkv_width:], upper[:share, qkv_width:]], 0)
    lower, upper = lower[:, :qkv_width], upper[:, :qkv_width]
    spare = jnp.zeros((-2 * (share + 1) % 8, qkv_width), low)
    full_qkv = pieces_along(
        "z",
        jnp.concatenate([lower[:share], upper[:share], lower[share:], upper[share:], spare], 0),
        zs,
    )

    own_gu = (
        gate_up_weight.astype(low)
        .reshape(share, 2, xs, 2, zs, ys * ff_share)
        .transpose(3, 1, 0, 4, 2, 5)
        .reshape(4, share, half)
    )
    quad = core * 2 + y_index
    quads = place(
        [pick(own_gu, quad)]
        + [swap(("core", "y"), pick(own_gu, quad ^ step), 4, step) for step in range(1, 4)],
        quad,
    ).reshape(2, 2 * share, half)
    first = jnp.concatenate([quads[0], pair_out], 1)
    full_qkv, first, second = hold(full_qkv, first, quads[1])
    first = pieces_along("z", first, zs)
    full_qkv = pieces_along("x", place_steps(full_qkv, z_index), xs)
    full_qkv, first, second = hold(full_qkv, first, second)
    second = pieces_along("z", second, zs)
    first = pieces_along("x", place(first, z_index), xs)
    full_qkv = gather_axis(place(full_qkv, x_index), "core", 2).swapaxes(0, 1)
    full_small = full_qkv[..., 2 * share : 2 * share + ys, :small_share].reshape(-1)
    full_qkv = full_qkv[..., : 2 * share, :].reshape(D, qkv_width)

    small_used = full_small.astype(jnp.float32)
    gain_attn = small_used[:D]
    gain_mlp = small_used[D : 2 * D]
    bias = small_used[2 * D :]
    state = inputs.reshape(tokens, D).astype(jnp.float32)
    inverse_attn = lax.rsqrt(jnp.mean(state * state, -1, keepdims=True) + EPS)
    normed = (state * inverse_attn * gain_attn).astype(low)
    qkv = across(full_qkv, normed, 0, 1) + bias[:, None]
    angles = rotation(positions, rows)
    query = (turn(qkv[:QD], angles, 1.0) * scale).astype(low)
    keys = turn(qkv[QD : QD + kv_width], angles, 1.0).astype(low)
    values = qkv[QD + kv_width :].astype(low)
    own_kv = jnp.concatenate(
        [keys.reshape(KVH, HD, tokens), values.reshape(KVH, HD, tokens)], 1
    ).transpose(0, 2, 1)
    own_kv = own_kv.reshape(KVH, rows, block_len, 2 * HD)

    valid = (positions[None, :] < lengths[:, None]).astype(jnp.float32)
    upstream = cotangent.reshape(tokens, D).astype(jnp.float32) * valid.reshape(tokens, 1)

    own_kv, second, down_weight, upstream = hold(own_kv, second, down_weight, upstream)
    full_down = lax.all_gather(down_weight.astype(low), ("z", "x", "y"), axis=0, tiled=True)
    all_kv = pieces_along("z", own_kv, zs, True)
    second = pieces_along("y", place(second, z_index), ys)
    all_kv, first, second, upstream = hold(all_kv, first, second, upstream)
    all_kv = pieces_along("y", place(all_kv, z_index), ys)
    second = pieces_along("x", place(second, y_index), xs)
    first = place(first, x_index)
    first, full_out = first[..., :half], first[..., half:]
    all_kv, first, full_out, upstream = hold(all_kv, first, full_out, upstream)
    all_kv = place(all_kv, y_index)
    full_out = gather_axis(full_out, "core", 2).swapaxes(0, 1).reshape(QD, D)
    first = pieces_along("y", first, ys)
    meta = jnp.concatenate([ctx_index.astype(jnp.int32).reshape(1), lengths])
    attended, logs = attention(meta, query, all_kv, block_len)
    attended, first, second = hold(attended, first, second)
    spot = jnp.stack([y_index, x_index]).astype(jnp.int32)
    slab = D // (2 * xs)
    first = [part.reshape(xs, slab, half) for part in first]
    second = [part.reshape(2, slab, half) for part in second]
    mixed_low = attended.astype(low)
    hidden_state = state + across(mixed_low, full_out, 0, 0)
    inverse_mlp = lax.rsqrt(jnp.mean(hidden_state * hidden_state, -1, keepdims=True) + EPS)
    normed2 = (hidden_state * inverse_mlp * gain_mlp).astype(low)

    def pair(value):
        return value, swap("core", value, 2, 1)

    def pair_sum(value):
        return value[:tokens] + swap("core", value[tokens:], 2, 1)

    pair_up = pair(upstream.astype(low))
    pair_normed = pair(normed2)
    inner, d_both, full_gate, full_up, features = hidden_part(
        spot, pair_normed, pair_up, first, second, full_down
    )

    middle = half // 256 // 2 * 256 + 128

    def exchange(parts):
        first, second = list(parts[:2]), list(parts[2:])
        first[1] = swap("y", first[1], ys, 1)
        return first, second[:1] + [swap("x", second[i], xs, i) for i in range(1, xs)]

    left = gate_up_grads(spot, features, d_both, xs, 0, middle, 384)
    *left, d_both, inner = hold(*left, d_both, inner)
    left = exchange(left)
    right = gate_up_grads(spot, features, d_both, xs, middle, half, 384)
    grad_down = down_grad(inner, pair_up, 512)
    left, right, grad_down, d_both, inner = hold(left, right, grad_down, d_both, inner)
    red_down = lax.psum_scatter(grad_down, "z", scatter_dimension=0, tiled=True)
    output = project(inner, full_down)
    right = exchange(right)
    d_normed2 = hidden_back(d_both, full_gate, full_up)
    left, right, d_normed2, output = hold(left, right, d_normed2, output)
    first = sums_of((left[0], right[0]), x_index, xs)
    second = sums_of((left[1], right[1]), y_index, ys)
    d_hidden, grad_gain_mlp, d_mixed, grad_out = norm_and_out_back(
        d_normed2[0],
        swap("core", d_normed2[1], 2, 1),
        hidden_state,
        upstream,
        inverse_mlp,
        gain_mlp,
        full_out,
        mixed_low,
    )
    grad_out = parts_along(
        "core", grad_out.reshape(xs, 2, zs, 2 * share, D), 1, 2
    )
    first, second, grad_out, d_mixed = hold(first, second, grad_out, d_mixed)
    first, second = send_parts("x", first), send_parts("y", second)
    d_query, kv_terms = [None] * KVH, [None] * KVH
    d_query[0], kv_terms[0] = attention_back(
        0, meta, query, d_mixed, attended, logs, all_kv, block_len
    )
    first, second, d_query[0], kv_terms[0], query = hold(
        first, second, d_query[0], kv_terms[0], query
    )
    red_quads = [add_up(part).reshape(zs, 2 * share, -1) for part in (first, second)]
    red_quads = parts_of(jnp.concatenate(red_quads, -1), z_index, 0, zs)
    grad_out = parts_of(add_up(grad_out), x_index, 0, xs)
    kv_terms[0] = parts_of(kv_terms[0], y_index, 0, ys)
    red_quads, grad_out, kv_terms[0], query = hold(red_quads, grad_out, kv_terms[0], query)
    red_quads, grad_out = send_parts("z", red_quads), send_parts("x", grad_out)
    kv_terms[0] = send_parts("y", kv_terms[0])
    d_query[1], kv_terms[1] = attention_back(
        1, meta, query, d_mixed, attended, logs, all_kv, block_len
    )
    red_quads, grad_out, kv_terms, d_query[1], red_down = hold(
        red_quads, grad_out, kv_terms, d_query[1], red_down
    )
    kv_terms[1] = parts_along("y", kv_terms[1], 0, ys)
    red_down = parts_along("x", red_down.reshape(xs, ys, ff_share, D), 0, xs)
    output = hidden_state + pair_sum(output)
    kv_terms, red_down, output, red_quads, grad_out = hold(
        kv_terms, red_down, output, red_quads, grad_out
    )
    kv_terms = jnp.stack([add_up(part) for part in kv_terms], 1)
    kv_terms = parts_along("z", kv_terms, 0, zs, True)
    kv_terms, red_quads, red_down, grad_out = hold(kv_terms, red_quads, red_down, grad_out)
    red_quads = add_up(red_quads)
    red_quads = jnp.stack([red_quads[:, :half], red_quads[:, half:]], 0)
    red_quads = parts_along("y", red_quads.reshape(2, ys, share, half), 1, ys)
    red_down = parts_along("y", add_up(red_down), 0, ys)
    red_out = parts_along("z", add_up(grad_out), 0, zs)
    kv_grads = total_of(kv_terms)
    red_gu = parts_along("core", place(red_quads, y_index), 1, 2)
    d_query = jnp.concatenate(d_query, 0)
    kv_grads = kv_grads.reshape(KVH, tokens, 2 * HD).transpose(0, 2, 1)
    d_qkv = jnp.concatenate(
        [
            turn(d_query * scale, angles, -1.0),
            turn(kv_grads[:, :HD].reshape(kv_width, tokens), angles, -1.0),
            kv_grads[:, HD:].reshape(kv_width, tokens),
        ],
        0,
    ).astype(low)
    grad_bias = jnp.sum(d_qkv.astype(jnp.float32), 1)
    grad_qkv = across(normed, d_qkv, 0, 1)
    d_normed = across(d_qkv, full_qkv, 0, 1)
    change_attn, grad_gain_attn = norm_back(state, inverse_attn, gain_attn, d_normed)
    input_grad = (d_hidden + change_attn).astype(low)
    grad_small = jnp.concatenate([grad_gain_attn, grad_gain_mlp[0], grad_bias])

    grad_small = grad_small.astype(low).reshape(-1, ys, small_share)
    grad_small = jnp.pad(grad_small, ((0, 0), (0, 8 - ys), (0, qkv_width - small_share)))
    grad_qkv = jnp.concatenate(
        [grad_qkv.astype(low).reshape(-1, ys * share, qkv_width), grad_small], 1
    )
    red_qkv = grad_qkv.reshape(xs, 2, zs, -1, qkv_width)
    red_qkv = add_up(parts_along("core", red_qkv, 1, 2))
    red_qkv = parts_along("x", red_qkv, 0, xs)
    red_qkv, red_gu, red_out, red_down = hold(red_qkv, red_gu, red_out, red_down)
    red_out = add_up(red_out)
    red_qkv = add_up(parts_along("z", add_up(red_qkv), 0, zs))
    red_down = total_of(red_down)

    red_small = red_qkv[ys * share : ys * share + ys]
    red_qkv = red_qkv[: ys * share].reshape(ys, share, qkv_width)
    red_out = red_out.reshape(ys, share, D)
    along = jnp.zeros((ys, -share % 8, qkv_width + D), low)
    along = along.at[:, 0, :qkv_width].set(red_small)
    along = jnp.concatenate([jnp.concatenate([red_qkv, red_out], 2), along], 1)
    mine = pick(along, y_index).astype(jnp.float32)
    mine = mine + swap("y", pick(along, 1 - y_index), ys, 1).astype(jnp.float32)
    red_qkv, red_out = mine[:share, :qkv_width], mine[:share, qkv_width:]
    red_small = mine[share, :small_share]
    red_gu = place(red_gu, core)
    red_gu = (
        red_gu.reshape(2, 2, share, zs, xs, ys * ff_share)
        .transpose(2, 1, 4, 0, 3, 5)
        .reshape(share, 2 * FF)
        .astype(jnp.float32)
    )

    red_gu, red_qkv, red_out, red_small = hold(red_gu, red_qkv, red_out, red_small)
    local_square = (
        jnp.sum(red_qkv * red_qkv)
        + jnp.sum(red_out * red_out)
        + jnp.sum(red_gu * red_gu)
        + jnp.sum(red_down * red_down)
        + jnp.sum(red_small * red_small)
    ).reshape(1)
    square_sum = local_square
    for axis, count in (("core", 2), ("y", ys), ("x", xs), ("z", zs)):
        square_sum = tree_sum(square_sum, axis, count)
    square_sum = square_sum[0]
    grad_norm = jnp.sqrt(square_sum)
    factor = CLIP / jnp.maximum(grad_norm, CLIP)
    qkv_new = adam_step(red_qkv, qkv_moment, qkv_square, qkv_weight, factor, RATES[0], DECAYS[0])
    out_new = adam_step(red_out, out_moment, out_square, out_weight, factor, RATES[1], DECAYS[1])
    gu_new = adam_step(
        red_gu, gate_up_moment, gate_up_square, gate_up_weight, factor, RATES[2], DECAYS[2]
    )
    down_new = adam_step(
        red_down, down_moment, down_square, down_weight, factor, RATES[3], DECAYS[3]
    )
    small_new = adam_step(
        red_small, small_moment, small_square, gains_biases, factor, RATES[4], DECAYS[4]
    )
    return (
        output.astype(low).reshape(inputs.shape),
        input_grad.reshape(inputs.shape),
        grad_norm,
        *qkv_new,
        *out_new,
        *gu_new,
        *down_new,
        *small_new,
    )


def solution(mesh):
    dp, ctx = mesh.shape["dp"], mesh.shape["ctx"]
    sizes = (dp // 2, ctx // 2, 2)
    fine = Mesh(mesh.devices.reshape(dp // 2, 2, ctx // 2, 2), ("x", "core", "z", "y"))
    seqs, blocks = ("x", "core"), ("z", "y")
    token = P(seqs, blocks, None)
    matrix = P(seqs + blocks, None)
    vector = P(seqs + blocks)
    weights = (matrix,) * 4 + (vector,)
    states = (matrix,) * 8 + (vector,) * 2
    return jax.shard_map(
        functools.partial(layer, sizes),
        mesh=fine,
        in_specs=(token, token, P(seqs)) + weights + states,
        out_specs=(token, token, P()) + (matrix,) * 16 + (vector,) * 4,
        check_vma=False,
    )
```
